256 devices in a mesh: row: 32 (over z_lo, x, core), col: 4 (over y), depth: 2 (over z_hi).
Axes of the slice: x: 4, y: 4, z: 8 (z_hi: 2, z_lo: 4; z = z_hi * 4 + z_lo), core: 2. Of those that a mesh axis runs over, the one named last changes fastest.
Arguments:
- queries: bfloat16 [4608, 4096], P('row'), may hold values from -34 to 34, as said below
- key_states: bfloat16 [4608, 4096], P(('col', 'depth'), 'row'), may hold values from -8 to 8
- value_states: bfloat16 [4608, 4096], P(('col', 'depth'), 'row'), may hold values from -6 to 6
- grad_output: bfloat16 [4608, 4096], P('row'), may hold values from -6 to 6
- bias_table: float32 [32, 64], replicated, may hold values from -4 to 4
- gap_bucket: int32 [4608], P(('col', 'depth')), may hold values from 0 to 63
- block_order: int32 [64], replicated, may hold values from 0 to 63, as said below
Outputs:
- grad_queries: float32 [4608, 4096], P('row', ('col', 'depth'))
- grad_keys: float32 [4608, 4096], P(('col', 'depth'), 'row')
- grad_values: float32 [4608, 4096], P(('col', 'depth'), 'row')
- grad_bias: float32 [32, 64], P('row')
The draws below stay inside these ranges and needn't reach their ends.
Inputs may be any that keep to these rules, and one draw needn't show every extreme that they name: `queries`: drawn afresh for each run; some query rows may be long and nearly aligned with a few keys. `block_order`: A permutation of the 64 blocks in which stored blocks 2 r and 2 r + 1 hold causal blocks k and 63 - k, in either order, for some k.
All inputs are finite; a program needn't handle non-finite values.
Results may differ from the reference program's by a relative error of at most 0.008.
Values may be sent and summed in bfloat16 or wider, within the bound.
A program may use at most 128 MiB of HBM per device.

```python
import jax
import jax.numpy as jnp
from jax import lax

HEADS = 32
HEAD_DIM = 128
BUCKETS = 64
ROWS_DEV = 144
EVENTS = 4608
ROW_BLOCKS = 64


def draw_queries(key, part):
    key = jax.random.fold_in(key, 1)
    base_key = jax.random.fold_in(key, 0)
    base = jax.random.normal(base_key, (EVENTS, HEADS, HEAD_DIM), jnp.float32)
    return base.reshape(EVENTS, HEADS * HEAD_DIM).astype(jnp.bfloat16)


def draw_key_states(key, part):
    key = jax.random.fold_in(key, 2)
    base_key = jax.random.fold_in(key, 0)
    base = jax.random.normal(base_key, (EVENTS, HEADS, HEAD_DIM), jnp.float32)
    return base.reshape(EVENTS, HEADS * HEAD_DIM).astype(jnp.bfloat16)


def draw_block_order(key, part):
    key = jax.random.fold_in(key, 3)
    pair_key, flip_key = jax.random.split(key, 2)
    half_count = ROW_BLOCKS // 2
    low_blocks = jax.random.permutation(pair_key, jnp.arange(half_count, dtype=jnp.int32))
    high_blocks = ROW_BLOCKS - 1 - low_blocks
    flipped = jax.random.randint(flip_key, (half_count,), 0, 2, dtype=jnp.int32)
    first_block = jnp.where(flipped == 1, high_blocks, low_blocks)
    second_block = jnp.where(flipped == 1, low_blocks, high_blocks)
    return jnp.stack([first_block, second_block], axis=1).reshape(ROW_BLOCKS).astype(jnp.int32)


def with_ends(entries, stream_key, low, top_value):
    longest = entries.shape.index(max(entries.shape))
    spots = []
    for shift in (0, 1):
        where = [jax.random.randint(jax.random.fold_in(stream_key, axis), (), 0, length) for axis, length in enumerate(entries.shape)]
        where[longest] = (where[longest] + shift) % entries.shape[longest]
        spots.append(tuple(where))
    return entries.at[spots[0]].set(low).at[spots[1]].set(top_value)


def block_levels(own_key, extent, pieces, least, top_value):
    def one(position, blocks):
        steps = jax.random.uniform(jax.random.fold_in(jax.random.fold_in(own_key, 6), position), (blocks,), jnp.float32, least / len(pieces), top_value / len(pieces))
        return jnp.repeat(jnp.exp(steps), extent[position] // blocks).reshape((-1,) + (1,) * (len(extent) - position - 1))

    gain = one(*pieces[0])
    for cut in pieces[1:]:
        gain = gain * one(*cut)
    return gain


def normal_values(rng, extent, width, limit, shards=(), kind=jnp.bfloat16):
    array = width * jax.random.normal(rng, extent, jnp.float32)
    if shards:
        array = array * block_levels(rng, extent, shards, -0.22, 0.18)
    return jnp.clip(array, -limit, limit).astype(kind)


def setup_inputs(seed: int = 0) -> dict:
    seeds = jax.random.split(jax.random.key(seed), 8)
    return {
        "queries": draw_queries(jax.random.fold_in(seeds[7], 71), 0),
        "key_states": draw_key_states(jax.random.fold_in(seeds[7], 71), 0),
        "value_states": normal_values(seeds[2], (EVENTS, HEADS * HEAD_DIM), 1.0, 6.0, ((0, 8), (1, 32))),
        "grad_output": normal_values(seeds[3], (EVENTS, HEADS * HEAD_DIM), 1.0, 6.0, ((0, 32),)),
        "bias_table": normal_values(seeds[4], (HEADS, BUCKETS), 1.0, 4.0, (), jnp.float32),
        "gap_bucket": with_ends(jax.random.randint(seeds[5], (EVENTS,), 0, BUCKETS), jax.random.fold_in(seeds[5], 1), 0, BUCKETS - 1).astype(jnp.int32),
        "block_order": draw_block_order(jax.random.fold_in(seeds[7], 71), 0),
    }


masked_value = -1.0e30


def reference(queries, key_states, value_states, grad_output, bias_table, gap_bucket, block_order):
    block_rows = ROWS_DEV // 2
    events = jnp.arange(EVENTS, dtype=jnp.int32)
    query_pos = block_order[events // block_rows] * block_rows + events % block_rows
    visible = events[None, :] <= query_pos[:, None]
    levels = jnp.arange(BUCKETS, dtype=jnp.int32)
    onehot = (gap_bucket[:, None] == levels[None, :]).astype(jnp.float32)
    score_scale = HEAD_DIM ** -0.5

    def split_heads(whole):
        return whole.reshape(EVENTS, HEADS, HEAD_DIM).transpose(1, 0, 2)

    def one_head(items):
        query_head, key_head, value_head, grad_head, table_row = items
        bias_row = jnp.dot(onehot, table_row, precision=lax.Precision.HIGHEST)
        scores = jnp.dot(query_head, key_head.T, preferred_element_type=jnp.float32) * score_scale + bias_row[None, :]
        scores = jnp.where(visible, scores, masked_value)
        row_max = jnp.max(scores, axis=1)
        weights = jnp.where(visible, jnp.exp(scores - row_max[:, None]), 0.0)
        row_lse = row_max + jnp.log(jnp.sum(weights, axis=1))
        attention = jnp.where(visible, jnp.exp(scores - row_lse[:, None]), 0.0)
        grad_probs = jnp.dot(grad_head, value_head.T, preferred_element_type=jnp.float32)
        delta = jnp.sum(attention * grad_probs, axis=1)
        grad_scores = attention * (grad_probs - delta[:, None])
        grad_low = grad_scores.astype(jnp.bfloat16)
        attention_low = attention.astype(jnp.bfloat16)
        query_grad = jnp.dot(grad_low, key_head, preferred_element_type=jnp.float32) * score_scale
        key_grad = jnp.dot(grad_low.T, query_head, preferred_element_type=jnp.float32) * score_scale
        value_grad = jnp.dot(attention_low.T, grad_head, preferred_element_type=jnp.float32)
        bias_grad = jnp.dot(jnp.sum(grad_scores, axis=0), onehot, precision=lax.Precision.HIGHEST)
        return query_grad, key_grad, value_grad, bias_grad

    query_grad, key_grad, value_grad, bias_grad = lax.map(one_head, (split_heads(queries), split_heads(key_states), split_heads(value_states), split_heads(grad_output), bias_table))

    def join_heads(per_head):
        return per_head.transpose(1, 0, 2).reshape(EVENTS, HEADS * HEAD_DIM).astype(jnp.float32)

    return join_heads(query_grad), join_heads(key_grad), join_heads(value_grad), bias_grad
```

```python
import functools
import math

import jax
import jax.numpy as jnp
from jax import lax
from jax.experimental import pallas as pl
from jax.experimental.pallas import tpu as pltpu
from jax.sharding import PartitionSpec as P

rows = 144
dim = 128
keys = 576
both = 2 * keys
levels = 64
slots = 16
queries = slots * rows
cuts = (0, 512, 1152, 1664, 2304)
z_steps = (0, 1, 3, 2)
tile = 384
tiles = both // tile
scale = dim ** -0.5
log2e = math.log2(math.e)
masked_value = -1e30
floor_value = -1e20
MESH = pl.DeviceIdType.MESH


def fold(a, combine):
    return combine(a.reshape(a.shape[0] // 8, 8, a.shape[1]), axis=0)


def wide(a, count):
    return jnp.concatenate([a] * count, axis=1)


def nt_dot(a, b):
    return lax.dot_general(a, b, (((1,), (1,)), ((), ())), preferred_element_type=jnp.float32)


def nn_dot(a, b):
    return jnp.dot(a, b, preferred_element_type=jnp.float32)


def column_of(row):
    pieces = []
    eye = lax.broadcasted_iota(jnp.int32, (dim, dim), 0) == lax.broadcasted_iota(
        jnp.int32, (dim, dim), 1
    )
    for start in range(0, keys, dim):
        spread = jnp.broadcast_to(row[:, start : start + dim], (dim, dim))
        column = jnp.sum(jnp.where(eye, spread, 0.0), axis=1, keepdims=True)
        pieces.append(column[: min(dim, keys - start)])
    return jnp.concatenate(pieces, axis=0)


def kernel(
    q_ref,
    g_ref,
    k_ref,
    v_ref,
    table_ref,
    gap_ref,
    order_ref,
    dq_out,
    dk_out,
    dv_out,
    db_out,
    q_all,
    g_all,
    k_all,
    v_all,
    k_turned,
    gap_own,
    gap_got,
    gap_cols,
    bias_cols,
    key_pos,
    query_pos,
    s_all,
    dp_all,
    stats,
    stats_got,
    dq_turned,
    dq_all,
    dq_got,
    dk_sum,
    dv_sum,
    ds_sum,
    dk_low,
    dv_low,
    dk_got,
    dv_got,
    db_own,
    db_got,
    kv_send,
    kv_recv,
    q_send,
    q_recv,
    g_send,
    g_recv,
    st_send,
    st_recv,
    dq_send,
    dq_recv,
    dkv_send,
    dkv_recv,
    db_send,
    db_recv,
):
    row = lax.axis_index("row")
    col = lax.axis_index("col")
    depth = lax.axis_index("depth")
    z_lo = row // 8
    x = (row // 2) % 4
    core = row % 2
    z = depth * 4 + z_lo
    member = col // 2
    other = (core + member) % 2
    partner = 3 - col
    own_row = member == 0
    dq_self = (member == 0) & (col == z_lo) & (depth == x // 2)

    def at(step, xx):
        there = (z + step + 8) % 8
        return ((there % 4) * 8 + xx * 2 + other, col, there // 4)

    def dq_target(j, xx):
        return (((z_lo + z_steps[j]) % 4) * 8 + xx * 2 + other, z_lo, x // 2)

    def peer(a, b):
        return (row, (col + a) % 4, (depth + b) % 2)

    def stat_peer(a, b):
        return (row, member * 2 + (col + a) % 2, (depth + b) % 2)

    barrier = pltpu.get_barrier_semaphore()

    def greet(device):
        pl.semaphore_signal(barrier, inc=1, device_id=device, device_id_type=MESH)

    for step in (0, 1, -1, 2, -2):

        def greet_row(i, carry, step=step):
            if step == 0:

                @pl.when(jnp.logical_not(own_row & (i == x)))
                def _():
                    greet(at(step, i))

            else:
                greet(at(step, i))
            return carry

        lax.fori_loop(0, 4, greet_row, 0)

    for n in range(1, 8):
        greet(peer(n // 2, n % 2))

    def greet_source(i, carry):
        head_x = depth * 2 + i // 8
        head_core = (i // 4) % 2
        source_col = ((head_core + core) % 2) * 2 + (i // 2) % 2
        is_self = dq_self & (head_x == x) & (head_core == core) & (source_col == col) & (
            i % 2 == depth
        )

        @pl.when(jnp.logical_not(is_self))
        def _():
            greet((col * 8 + head_x * 2 + head_core, source_col, i % 2))

        return carry

    lax.fori_loop(0, slots, greet_source, 0)

    gap_own[...] = jnp.zeros_like(gap_own)
    gap_own[0:1, 0:keys] = gap_ref[...].astype(jnp.float32)
    k_all[0:keys, :] = k_ref[...]
    v_all[0:keys, :] = v_ref[...]

    expected = 20 + 7 + 16 - own_row.astype(jnp.int32) - dq_self.astype(jnp.int32)
    pl.semaphore_wait(barrier, expected)

    mate = (row, partner, depth)
    exchange = [
        pltpu.make_async_remote_copy(
            src_ref=src,
            dst_ref=dst,
            send_sem=kv_send.at[n],
            recv_sem=kv_recv.at[n],
            device_id=mate,
            device_id_type=MESH,
        )
        for n, (src, dst) in enumerate(
            (
                (gap_own, gap_got),
                (k_ref, k_all.at[pl.ds(keys, keys), :]),
                (v_ref, v_all.at[pl.ds(keys, keys), :]),
            )
        )
    ]
    for copy in exchange:
        copy.start()

    def send_rows(src, dst, send_sem, recv_sem, step, j):
        def one(i, carry):
            xx = (x + i) % 4
            target = at(step, xx)
            src_part = src.at[:, pl.ds(pl.multiple_of(target[0] * dim, dim), dim)]
            dst_part = dst.at[pl.ds(pl.multiple_of((j * 4 + x) * rows, rows), rows), :]

            def remote():
                pltpu.make_async_remote_copy(
                    src_ref=src_part,
                    dst_ref=dst_part,
                    send_sem=send_sem,
                    recv_sem=recv_sem.at[j],
                    device_id=target,
                    device_id_type=MESH,
                ).start()

            if step == 0:
                mine = own_row & (i == 0)

                @pl.when(mine)
                def _():
                    pltpu.make_async_copy(src_part, dst_part, recv_sem.at[j]).start()

                @pl.when(jnp.logical_not(mine))
                def _():
                    remote()

            else:
                remote()
            return carry

        lax.fori_loop(0, 4, one, 0)

    for step, j in ((0, 0), (-1, 1), (1, 2)):
        send_rows(q_ref, q_all, q_send, q_recv, step, j)
        send_rows(g_ref, g_all, g_send, g_recv, step, j)
    send_rows(q_ref, q_all, q_send, q_recv, -2, 3)
    send_rows(g_ref, g_all, g_send, g_recv, 2, 3)

    lane = lax.broadcasted_iota(jnp.int32, (1, queries), 1)
    half = rows // 2

    def place(b, pos):
        slot = b // 2
        j = slot // 4
        step = j + (j // 2) * (1 - 2 * (j % 2))
        r = ((z_lo + step) % 4) * 8 + (slot % 4) * 2 + other
        first = order_ref[2 * r + b % 2] * half
        inside = (lane >= b * half) & (lane < b * half + half)
        return jnp.where(inside, first + lane - b * half, pos)

    query_pos[...] = lax.fori_loop(0, 2 * slots, place, jnp.zeros((1, queries), jnp.int32))
    block = col * 2 + depth
    partner_block = partner * 2 + depth
    within = lax.broadcasted_iota(jnp.int32, (keys, dim), 0)
    key_pos[0:keys, :] = within + block * keys
    key_pos[keys:both, :] = within + partner_block * keys
    level = lax.broadcasted_iota(jnp.int32, (1, levels), 1).astype(jnp.float32)
    table = table_ref[pl.ds(row, 1), :]

    def fill_bias(gap, start):
        column = column_of(gap)
        gap_cols[start : start + keys, :] = jnp.broadcast_to(column, (keys, dim))
        bias = jnp.sum(jnp.where(column == level, table, 0.0), axis=1, keepdims=True)
        bias_cols[start : start + keys, :] = jnp.broadcast_to(bias * log2e, (keys, dim))

    fill_bias(gap_own[0:1, :], 0)
    dk_sum[...] = jnp.zeros_like(dk_sum)
    dv_sum[...] = jnp.zeros_like(dv_sum)
    ds_sum[...] = jnp.zeros_like(ds_sum)
    for copy in exchange:
        copy.wait()
    fill_bias(gap_got[0:1, :], keys)
    for t in range(tiles):
        part = k_all[t * tile : (t + 1) * tile, :].astype(jnp.float32)
        k_turned[t] = part.T.astype(jnp.bfloat16)

    def wait_group(buffer, sem, j):
        part = buffer.at[pl.ds(j * 4 * rows, 4 * rows), :]
        pltpu.make_async_copy(part, part, sem.at[j]).wait()

    def stat_copy(c, n):
        lo, hi = cuts[c], cuts[c + 1]
        return pltpu.make_async_remote_copy(
            src_ref=stats.at[:, pl.ds(lo, hi - lo)],
            dst_ref=stats_got.at[n - 1, :, pl.ds(lo, hi - lo)],
            send_sem=st_send.at[c, n - 1],
            recv_sem=st_recv.at[c, n - 1],
            device_id=stat_peer(n // 2, n % 2),
            device_id_type=MESH,
        )

    for c in range(4):
        lo, hi = cuts[c], cuts[c + 1]
        count = hi - lo
        wait_group(q_all, q_recv, c)
        pos = query_pos[:, lo:hi]
        q_part = q_all[lo:hi, :]

        def scores(t, best):
            start = pl.multiple_of(t * tile, tile)
            part = pl.ds(start, tile)
            s = nt_dot(k_all[part, :], q_part) * (scale * log2e)
            s = s + wide(bias_cols[part, :], count // dim)
            s = jnp.where(wide(key_pos[part, :], count // dim) <= pos, s, masked_value)
            s_all[part, lo:hi] = s
            return jnp.maximum(best, fold(s, jnp.max))

        best = lax.fori_loop(0, tiles, scores, jnp.full((8, count), masked_value, jnp.float32))
        best = jnp.maximum(jnp.max(best, axis=0, keepdims=True), floor_value)
        wait_group(g_all, g_recv, c)
        g_part = g_all[lo:hi, :]

        def sums(t, state):
            start = pl.multiple_of(t * tile, tile)
            part = pl.ds(start, tile)
            dp = nt_dot(v_all[part, :], g_part)
            dp_all[part, lo:hi] = dp
            w = jnp.exp2(s_all[part, lo:hi] - best)
            return state[0] + fold(w, jnp.sum), state[1] + fold(w * dp, jnp.sum)

        zero = jnp.zeros((8, count), jnp.float32)
        total, moment = lax.fori_loop(0, tiles, sums, (zero, zero))
        stats[0:1, lo:hi] = best
        stats[1:2, lo:hi] = jnp.sum(total, axis=0, keepdims=True)
        stats[2:3, lo:hi] = jnp.sum(moment, axis=0, keepdims=True)
        for n in range(1, 4):
            stat_copy(c, n).start()

    sent = 0
    for c in range(4):
        lo, hi = cuts[c], cuts[c + 1]
        count = hi - lo
        for n in range(1, 4):
            stat_copy(c, n).wait()
        parts = [stats[0:3, lo:hi]] + [stats_got[n, 0:3, lo:hi] for n in range(3)]
        best = functools.reduce(jnp.maximum, [a[0:1] for a in parts])
        factors = [jnp.exp2(a[0:1] - best) for a in parts]
        total = sum(a[1:2] * f for a, f in zip(parts, factors))
        moment = sum(a[2:3] * f for a, f in zip(parts, factors))
        lse = best + jnp.log(total) * log2e
        delta = moment / total
        q_part = q_all[lo:hi, :]
        g_part = g_all[lo:hi, :]
        dq_turned[...] = jnp.zeros_like(dq_turned)

        def grads(t, carry):
            start = pl.multiple_of(t * tile, tile)
            part = pl.ds(start, tile)
            p = jnp.exp2(s_all[part, lo:hi] - lse)
            ds = p * (dp_all[part, lo:hi] - delta)
            ds_sum[part, :] += sum(
                ds[:, n * dim : (n + 1) * dim] for n in range(count // dim)
            )
            ds_low = ds.astype(jnp.bfloat16)
            dv_sum[part, :] += nn_dot(p.astype(jnp.bfloat16), g_part)
            dk_sum[part, :] += nn_dot(ds_low, q_part)
            dq_turned[:, 0:count] += nn_dot(k_turned[t], ds_low)
            return carry

        lax.fori_loop(0, tiles, grads, 0)
        dq_all[lo:hi, :] = (dq_turned[:, 0:count].T * scale).astype(jnp.bfloat16)
        while (sent + 1) * rows <= hi:
            j, xx = sent // 4, sent % 4
            src = dq_all.at[pl.ds(sent * rows, rows), :]
            place_at = ((x % 2) * 2 + core) * 4 + (col % 2) * 2 + depth
            dst = dq_got.at[place_at]

            def remote(j=j, xx=xx, src=src):
                pltpu.make_async_remote_copy(
                    src_ref=src,
                    dst_ref=dst,
                    send_sem=dq_send,
                    recv_sem=dq_recv,
                    device_id=dq_target(j, xx),
                    device_id_type=MESH,
                ).start()

            if j == 0:
                mine = dq_self & (x == xx)

                @pl.when(mine)
                def _(src=src):
                    pltpu.make_async_copy(src, dst, dq_recv).start()

                @pl.when(jnp.logical_not(mine))
                def _(remote=remote):
                    remote()

            else:
                remote()
            sent += 1

    dk_low[...] = (dk_sum[keys:both, :] * scale).astype(jnp.bfloat16)
    dv_low[...] = dv_sum[keys:both, :].astype(jnp.bfloat16)
    returns = [
        pltpu.make_async_remote_copy(
            src_ref=src,
            dst_ref=dst,
            send_sem=dkv_send.at[n],
            recv_sem=dkv_recv.at[n],
            device_id=mate,
            device_id_type=MESH,
        )
        for n, (src, dst) in enumerate(((dk_low, dk_got), (dv_low, dv_got)))
    ]
    for copy in returns:
        copy.start()

    column = jnp.sum(ds_sum[...], axis=1, keepdims=True)
    by_level = jnp.where(gap_cols[:, 0:levels] == level, column, 0.0)
    db_own[...] = jnp.zeros_like(db_own)
    db_own[0:1, 0:levels] = jnp.sum(by_level, axis=0, keepdims=True)
    biases = [
        pltpu.make_async_remote_copy(
            src_ref=db_own,
            dst_ref=db_got.at[n - 1],
            send_sem=db_send.at[n - 1],
            recv_sem=db_recv.at[n - 1],
            device_id=peer(n // 2, n % 2),
            device_id_type=MESH,
        )
        for n in range(1, 8)
    ]
    for copy in biases:
        copy.start()

    for copy in returns:
        copy.wait()
    dk_out[...] = dk_sum[0:keys, :] * scale + dk_got[...].astype(jnp.float32)
    dv_out[...] = dv_sum[0:keys, :] + dv_got[...].astype(jnp.float32)
    for copy in biases:
        copy.wait()
    db_out[...] = db_own[0:1, 0:levels] + sum(db_got[n, 0:1, 0:levels] for n in range(7))

    pltpu.make_async_copy(dq_got, dq_got, dq_recv).wait()
    for head in range(4):
        dq_out[:, head * dim : (head + 1) * dim] = sum(
            dq_got[head * 4 + n].astype(jnp.float32) for n in range(4)
        )

    def drain(buffer, sem, short):
        @pl.when(short)
        def _():
            part = buffer.at[pl.ds(0, queries - rows), :]
            pltpu.make_async_copy(part, part, sem).wait()

        @pl.when(jnp.logical_not(short))
        def _():
            pltpu.make_async_copy(buffer, buffer, sem).wait()

    drain(q_all, q_send, own_row)
    drain(g_all, g_send, own_row)
    drain(dq_all, dq_send, dq_self)


def per_device(queries_in, key_states, value_states, grad_output, bias_table, gap_bucket, order):
    vmem = pl.BlockSpec(memory_space=pltpu.VMEM)
    anywhere = pl.BlockSpec(memory_space=pl.ANY)
    low, full = jnp.bfloat16, jnp.float32
    dma = pltpu.SemaphoreType.DMA
    return pl.pallas_call(
        kernel,
        out_shape=(
            jax.ShapeDtypeStruct((rows, 4 * dim), full),
            jax.ShapeDtypeStruct((keys, dim), full),
            jax.ShapeDtypeStruct((keys, dim), full),
            jax.ShapeDtypeStruct((1, levels), full),
        ),
        in_specs=[
            anywhere,
            anywhere,
            vmem,
            vmem,
            vmem,
            vmem,
            pl.BlockSpec(memory_space=pltpu.SMEM),
        ],
        out_specs=(vmem, vmem, vmem, vmem),
        scratch_shapes=[
            pltpu.VMEM((queries, dim), low),
            pltpu.VMEM((queries, dim), low),
            pltpu.VMEM((both, dim), low),
            pltpu.VMEM((both, dim), low),
            pltpu.VMEM((tiles, dim, tile), low),
            pltpu.VMEM((8, 640), full),
            pltpu.VMEM((8, 640), full),
            pltpu.VMEM((both, dim), full),
            pltpu.VMEM((both, dim), full),
            pltpu.VMEM((both, dim), jnp.int32),
            pltpu.VMEM((1, queries), jnp.int32),
            pltpu.VMEM((both, queries), full),
            pltpu.VMEM((both, queries), full),
            pltpu.VMEM((8, queries), full),
            pltpu.VMEM((3, 8, queries), full),
            pltpu.VMEM((dim, 640), full),
            pltpu.VMEM((queries, dim), low),
            pltpu.VMEM((slots, rows, dim), low),
            pltpu.VMEM((both, dim), full),
            pltpu.VMEM((both, dim), full),
            pltpu.VMEM((both, dim), full),
            pltpu.VMEM((keys, dim), low),
            pltpu.VMEM((keys, dim), low),
            pltpu.VMEM((keys, dim), low),
            pltpu.VMEM((keys, dim), low),
            pltpu.VMEM((8, dim), full),
            pltpu.VMEM((7, 8, dim), full),
            dma((3,)),
            dma((3,)),
            dma(()),
            dma((4,)),
            dma(()),
            dma((4,)),
            dma((4, 3)),
            dma((4, 3)),
            dma(()),
            dma(()),
            dma((2,)),
            dma((2,)),
            dma((7,)),
            dma((7,)),
        ],
        compiler_params=pltpu.CompilerParams(
            collective_id=0, has_side_effects=True, vmem_limit_bytes=48 * 1024 * 1024
        ),
        cost_estimate=pl.CostEstimate(
            flops=10 * both * queries * dim,
            bytes_accessed=8 * queries * dim,
            transcendentals=2 * both * queries,
        ),
    )(
        queries_in,
        grad_output,
        key_states,
        value_states,
        bias_table,
        gap_bucket.reshape(1, keys),
        order,
    )


def solution(mesh):
    placed = (
        P("row", None),
        P(("col", "depth"), "row"),
        P(("col", "depth"), "row"),
        P("row", None),
        P(),
        P(("col", "depth")),
        P(),
    )
    return jax.shard_map(
        per_device,
        mesh=mesh,
        in_specs=placed,
        out_specs=(
            P("row", ("col", "depth")),
            P(("col", "depth"), "row"),
            P(("col", "depth"), "row"),
            P("row", None),
        ),
        check_vma=False,
    )
```

```python
import functools
import math

import jax
import jax.numpy as jnp
from jax import lax
from jax.experimental import pallas as pl
from jax.experimental.pallas import tpu as pltpu
from jax.sharding import PartitionSpec as P

rows = 144
dim = 128
keys = 576
blocks = 4
all_keys = blocks * keys
levels = 64
slots = 8
queries = slots * rows
chunk = 384
chunks = queries // chunk
z_steps = (0, 1, 3, 2)
tile = 288
per_block = keys // tile
tiles = blocks * per_block
scale = dim ** -0.5
log2e = math.log2(math.e)
masked_value = -1e30
floor_value = -1e20
MESH = pl.DeviceIdType.MESH


def fold(a, combine):
    return combine(a.reshape(a.shape[0] // 8, 8, a.shape[1]), axis=0)


def wide(a):
    return jnp.concatenate([a] * (chunk // dim), axis=1)


def nt_dot(a, b):
    return lax.dot_general(a, b, (((1,), (1,)), ((), ())), preferred_element_type=jnp.float32)


def nn_dot(a, b):
    return jnp.dot(a, b, preferred_element_type=jnp.float32)


def column_of(row):
    pieces = []
    eye = lax.broadcasted_iota(jnp.int32, (dim, dim), 0) == lax.broadcasted_iota(
        jnp.int32, (dim, dim), 1
    )
    for start in range(0, keys, dim):
        spread = jnp.broadcast_to(row[:, start : start + dim], (dim, dim))
        column = jnp.sum(jnp.where(eye, spread, 0.0), axis=1, keepdims=True)
        pieces.append(column[: min(dim, keys - start)])
    return jnp.concatenate(pieces, axis=0)


def merge(parts):
    best = functools.reduce(jnp.maximum, [a[0:1] for a in parts])
    factors = [jnp.exp2(a[0:1] - best) for a in parts]
    total = sum(a[1:2] * f for a, f in zip(parts, factors))
    moment = sum(a[2:3] * f for a, f in zip(parts, factors))
    return best, total, moment


def kernel(
    q_ref,
    g_ref,
    k_ref,
    v_ref,
    table_ref,
    gap_ref,
    order_ref,
    dq_out,
    dk_out,
    dv_out,
    db_out,
    q_all,
    g_all,
    k_all,
    v_all,
    k_turned,
    gap_rows,
    gap_cols,
    bias_cols,
    key_pos,
    query_pos,
    s_all,
    dp_all,
    part_stats,
    stats,
    stats_got,
    dq_turned,
    dq_all,
    mid_got,
    mid_low,
    fin_got,
    dk_sum,
    dv_sum,
    ds_sum,
    kv_low,
    kv_got,
    db_own,
    db_got,
    local_sem,
    gap_send,
    gap_recv,
    k_send,
    k_recv,
    v_send,
    v_recv,
    q_send,
    q_recv,
    g_send,
    g_recv,
    st_send,
    st_recv,
    dq_send,
    dq_recv,
    fin_send,
    fin_recv,
    dkv_send,
    dkv_recv,
    db_send,
    db_recv,
):
    row = lax.axis_index("row")
    col = lax.axis_index("col")
    depth = lax.axis_index("depth")
    z_lo = row // 8
    x = (row // 2) % 4
    core = row % 2
    z = depth * 4 + z_lo
    member = col // 2
    parity = col % 2
    other = (core + member) % 2
    own_row = col == 0
    mid_self = (col == 0) & (depth == x // 2)

    def shift(j):
        return (parity + (1 if j in (1, 2) else 0)) % 2

    def at(step, xx):
        there = (z + step + 8) % 8
        return ((there % 4) * 8 + xx * 2 + other, col, there // 4)

    def slot_x(s):
        return (x + shift(s // 2) + 2 * (s % 2)) % 4

    def peer(a, b):
        return (row, (col + a) % 4, (depth + b) % 2)

    barrier = pltpu.get_barrier_semaphore()

    def greet(device):
        pl.semaphore_signal(barrier, inc=1, device_id=device, device_id_type=MESH)

    for step, j in ((0, 0), (1, 1), (-1, 2), (2, 3), (-2, 3)):
        for i in range(2):
            device = at(step, (x + shift(j) + 2 * i) % 4)
            if step == 0 and i == 0:

                @pl.when(jnp.logical_not(own_row))
                def _(device=device):
                    greet(device)

            else:
                greet(device)
    for n in range(1, 8):
        greet(peer(n // 2, n % 2))
    for n in range(8):
        head_z, head_depth = n // 2, n % 2
        head_x = depth * 2 + (x + z_lo + 4 - head_z + parity) % 2

        @pl.when(jnp.logical_not(mid_self & (z_lo == head_z) & (depth == head_depth)))
        def _(head_z=head_z, head_depth=head_depth, head_x=head_x):
            greet((head_z * 8 + head_x * 2 + other, col, head_depth))

    own_k = pltpu.make_async_copy(k_ref, k_all.at[0], local_sem.at[0])
    own_v = pltpu.make_async_copy(v_ref, v_all.at[0], local_sem.at[1])
    own_k.start()
    own_v.start()
    gap_rows[0] = jnp.zeros((8, 640), jnp.float32)
    gap_rows[0, 0:1, 0:keys] = gap_ref[...].astype(jnp.float32).reshape(1, keys)

    pl.semaphore_wait(
        barrier, 25 - own_row.astype(jnp.int32) - mid_self.astype(jnp.int32)
    )

    def remote(src, dst, send_sem, recv_sem, device):
        return pltpu.make_async_remote_copy(
            src_ref=src,
            dst_ref=dst,
            send_sem=send_sem,
            recv_sem=recv_sem,
            device_id=device,
            device_id_type=MESH,
        )

    def gap_copy(a):
        return remote(
            gap_rows.at[0], gap_rows.at[4 - a], gap_send.at[a - 1], gap_recv.at[3 - a], peer(a, 0)
        )

    def own_copy(a, src, dst, send, recv):
        return remote(src, dst.at[4 - a], send.at[a - 1], recv.at[3 - a], peer(a, 0))

    def pass_copy(a, dst, send, recv):
        return remote(dst.at[4 - a], dst.at[2], send.at[1], recv.at[1], peer(a, 0))

    gaps = [gap_copy(a) for a in (1, 3, 2)]
    sides = [own_copy(a, k_ref, k_all, k_send, k_recv) for a in (1, 3)] + [
        own_copy(a, v_ref, v_all, v_send, v_recv) for a in (3, 1)
    ]
    k_pass = pass_copy(1, k_all, k_send, k_recv)
    v_pass = pass_copy(3, v_all, v_send, v_recv)
    for copy in (sides[0], sides[2]):
        copy.start()

    def send_rows(src, dst, send_sem, recv_sem, step, j):
        for i in range(2):
            target = at(step, (x + 3 * shift(j) + 2 * i) % 4)
            src_part = src.at[:, pl.ds(pl.multiple_of(target[0] * dim, dim), dim)]
            dst_part = dst.at[pl.ds((j * 2 + i) * rows, rows), :]
            away = remote(src_part, dst_part, send_sem, recv_sem.at[j], target)
            if step == 0 and i == 0:

                @pl.when(own_row)
                def _(src_part=src_part, dst_part=dst_part):
                    pltpu.make_async_copy(src_part, dst_part, recv_sem.at[j]).start()

                @pl.when(jnp.logical_not(own_row))
                def _(away=away):
                    away.start()

            else:
                away.start()

    send_rows(q_ref, q_all, q_send, q_recv, 0, 0)
    send_rows(g_ref, g_all, g_send, g_recv, 0, 0)
    for copy in gaps:
        copy.start()
    send_rows(q_ref, q_all, q_send, q_recv, -1, 1)
    send_rows(q_ref, q_all, q_send, q_recv, 1, 2)
    send_rows(q_ref, q_all, q_send, q_recv, -2, 3)
    send_rows(g_ref, g_all, g_send, g_recv, -1, 1)
    send_rows(g_ref, g_all, g_send, g_recv, 1, 2)
    send_rows(g_ref, g_all, g_send, g_recv, 2, 3)
    for copy in (sides[1], sides[3]):
        copy.start()

    lane = lax.broadcasted_iota(jnp.int32, (1, queries), 1)
    half = rows // 2
    pos = jnp.zeros((1, queries), jnp.int32)
    for s in range(slots):
        r = ((z_lo + z_steps[s // 2]) % 4) * 8 + slot_x(s) * 2 + other
        for b in range(2):
            low = s * rows + b * half
            inside = (lane >= low) & (lane < low + half)
            pos = jnp.where(inside, order_ref[2 * r + b] * half + lane - low, pos)
    query_pos[...] = pos
    within = lax.broadcasted_iota(jnp.int32, (keys, dim), 0)
    for b in range(blocks):
        key_pos[b * keys : (b + 1) * keys, :] = within + (((col + b) % 4) * 2 + depth) * keys
    level = lax.broadcasted_iota(jnp.int32, (1, levels), 1).astype(jnp.float32)
    table = table_ref[pl.ds(row, 1), :]

    def fill_bias(b):
        start = b * keys
        column = column_of(gap_rows[b, 0:1, :])
        gap_cols[start : start + keys, :] = jnp.broadcast_to(column, (keys, dim))
        bias = jnp.sum(jnp.where(column == level, table, 0.0), axis=1, keepdims=True)
        bias_cols[start : start + keys, :] = jnp.broadcast_to(bias * log2e, (keys, dim))

    def turn(b):
        for t in range(per_block):
            part = k_all[b, t * tile : (t + 1) * tile, :].astype(jnp.float32)
            k_turned[b * per_block + t] = part.T.astype(jnp.bfloat16)

    fill_bias(0)
    dk_sum[...] = jnp.zeros_like(dk_sum)
    dv_sum[...] = jnp.zeros_like(dv_sum)
    ds_sum[...] = jnp.zeros_like(ds_sum)
    own_k.wait()
    own_v.wait()
    turn(0)

    sides[0].wait_recv()
    k_pass.start()
    sides[2].wait_recv()
    v_pass.start()

    def wait_group(buffer, sem, j):
        part = buffer.at[pl.ds(j * 2 * rows, 2 * rows), :]
        pltpu.make_async_copy(part, part, sem.at[j]).wait()

    def first_pass(c, b):
        lo, hi = c * chunk, (c + 1) * chunk
        pos = query_pos[:, lo:hi]
        q_part = q_all[lo:hi, :]
        g_part = g_all[lo:hi, :]

        def scores(t, best):
            start = pl.multiple_of(t * tile, tile)
            part = pl.ds(pl.multiple_of(b * keys + start, tile), tile)
            s = nt_dot(k_all[b, pl.ds(start, tile), :], q_part) * (scale * log2e)
            s = s + wide(bias_cols[part, :])
            s = jnp.where(wide(key_pos[part, :]) <= pos, s, masked_value)
            s_all[part, lo:hi] = s
            return jnp.maximum(best, fold(s, jnp.max))

        best = lax.fori_loop(0, per_block, scores, jnp.full((8, chunk), masked_value, jnp.float32))
        best = jnp.maximum(jnp.max(best, axis=0, keepdims=True), floor_value)

        def sums(t, state):
            start = pl.multiple_of(t * tile, tile)
            part = pl.ds(pl.multiple_of(b * keys + start, tile), tile)
            dp = nt_dot(v_all[b, pl.ds(start, tile), :], g_part)
            dp_all[part, lo:hi] = dp
            w = jnp.exp2(s_all[part, lo:hi] - best)
            return state[0] + fold(w, jnp.sum), state[1] + fold(w * dp, jnp.sum)

        zero = jnp.zeros((8, chunk), jnp.float32)
        total, moment = lax.fori_loop(0, per_block, sums, (zero, zero))
        part_stats[b, 0:1, lo:hi] = best
        part_stats[b, 1:2, lo:hi] = jnp.sum(total, axis=0, keepdims=True)
        part_stats[b, 2:3, lo:hi] = jnp.sum(moment, axis=0, keepdims=True)

    def stat_copy(c):
        part = pl.ds(c * chunk, chunk)
        return remote(
            stats.at[:, part], stats_got.at[:, part], st_send.at[c], st_recv.at[c], peer(0, 1)
        )

    wait_group(q_all, q_recv, 0)
    wait_group(g_all, g_recv, 0)
    wait_group(q_all, q_recv, 1)
    wait_group(g_all, g_recv, 1)
    first_pass(0, 0)
    for copy in gaps:
        copy.wait_recv()
    for b in (3, 1, 2):
        fill_bias(b)
    sides[1].wait_recv()
    sides[3].wait_recv()
    turn(1)
    turn(3)
    first_pass(0, 1)
    first_pass(0, 3)
    for c in range(1, chunks):
        wait_group(q_all, q_recv, c + 1)
        wait_group(g_all, g_recv, c + 1)

        def near(i, carry, c=c):
            first_pass(c, i + i // 2)
            return carry

        lax.fori_loop(0, 3, near, 0)
    k_pass.wait_recv()
    v_pass.wait_recv()
    turn(2)
    for c in range(chunks):
        lo, hi = c * chunk, (c + 1) * chunk
        first_pass(c, 2)
        best, total, moment = merge([part_stats[b, 0:3, lo:hi] for b in range(blocks)])
        stats[0:1, lo:hi] = best
        stats[1:2, lo:hi] = total
        stats[2:3, lo:hi] = moment
        stat_copy(c).start()

    def kv_copy(n, a):
        return remote(
            kv_low.at[n], kv_got.at[n], dkv_send.at[n], dkv_recv.at[n], peer(a, 0)
        )

    returns = [kv_copy(n, a) for n, a in enumerate((1, 3, 3, 1, 1, 3))]

    def low(total, b, factor):
        return (total[b * keys : (b + 1) * keys, :] * factor).astype(jnp.bfloat16)

    sent = 0
    for c in range(chunks):
        lo, hi = c * chunk, (c + 1) * chunk
        stat_copy(c).wait()
        best, total, moment = merge([stats[0:3, lo:hi], stats_got[0:3, lo:hi]])
        lse = best + jnp.log(total) * log2e
        delta = moment / total
        q_part = q_all[lo:hi, :]
        g_part = g_all[lo:hi, :]
        dq_turned[...] = jnp.zeros_like(dq_turned)

        def grads(t, carry):
            start = pl.multiple_of(t * tile, tile)
            part = pl.ds(start, tile)
            p = jnp.exp2(s_all[part, lo:hi] - lse)
            ds = p * (dp_all[part, lo:hi] - delta)
            ds_sum[part, :] += sum(ds[:, n * dim : (n + 1) * dim] for n in range(chunk // dim))
            ds_low = ds.astype(jnp.bfloat16)
            dv_sum[part, :] += nn_dot(p.astype(jnp.bfloat16), g_part)
            dk_sum[part, :] += nn_dot(ds_low, q_part)
            dq_turned[...] += nn_dot(k_turned[t], ds_low)
            return carry

        if c < chunks - 1:
            lax.fori_loop(0, tiles, grads, 0)
        else:
            lax.fori_loop(2 * per_block, 3 * per_block, grads, 0)
            kv_low[0] = low(dk_sum, 2, scale)
            returns[0].start()
            kv_low[1] = low(dv_sum, 2, 1.0)
            returns[1].start()
            lax.fori_loop(3 * per_block, 4 * per_block, grads, 0)
            kv_low[2] = low(dk_sum, 3, scale)
            returns[2].start()
            lax.fori_loop(per_block, 2 * per_block, grads, 0)
            kv_low[3] = low(dv_sum, 1, 1.0)
            returns[3].start()
            lax.fori_loop(0, per_block, grads, 0)
        dq_all[lo:hi, :] = (dq_turned[...].T * scale).astype(jnp.bfloat16)
        while (sent + 1) * rows <= hi:
            j = sent // 2
            src = dq_all.at[pl.ds(sent * rows, rows), :]
            dst = mid_got.at[z_lo, pl.ds(pl.multiple_of(depth * rows, rows), rows), :]
            target = ((((z_lo + z_steps[j]) % 4) * 8 + slot_x(sent) * 2 + other), col, x // 2)
            away = remote(src, dst, dq_send, dq_recv.at[z_lo], target)
            if sent == 0:

                @pl.when(mid_self)
                def _(src=src, dst=dst):
                    pltpu.make_async_copy(src, dst, dq_recv.at[z_lo]).start()

                @pl.when(jnp.logical_not(mid_self))
                def _(away=away):
                    away.start()

            else:
                away.start()
            sent += 1

    column = jnp.sum(ds_sum[...], axis=1, keepdims=True)
    by_level = jnp.where(gap_cols[:, 0:levels] == level, column, 0.0)
    db_own[...] = jnp.zeros_like(db_own)
    db_own[0:1, 0:levels] = jnp.sum(by_level, axis=0, keepdims=True)
    biases = [
        remote(db_own, db_got.at[n - 1], db_send.at[n - 1], db_recv.at[n - 1], peer(n // 2, n % 2))
        for n in range(1, 8)
    ]
    for copy in biases:
        copy.start()

    returns[0].wait_recv()
    kv_low[4] = (dk_sum[keys : 2 * keys, :] * scale + kv_got[0].astype(jnp.float32)).astype(
        jnp.bfloat16
    )
    returns[4].start()
    returns[1].wait_recv()
    kv_low[5] = (dv_sum[3 * keys : 4 * keys, :] + kv_got[1].astype(jnp.float32)).astype(
        jnp.bfloat16
    )
    returns[5].start()

    def fin_copy(head_z, place):
        return remote(
            mid_low.at[head_z],
            fin_got.at[place],
            fin_send.at[head_z],
            fin_recv,
            (row, head_z, depth),
        )

    def place_of(head_z):
        return ((x + z_lo + 4 - head_z + parity) % 2) * 2 + other

    for head_z in range(4):
        both = mid_got.at[head_z]
        pltpu.make_async_copy(both, both, dq_recv.at[head_z]).wait()
        total = both[0:rows, :].astype(jnp.float32) + both[rows : 2 * rows, :].astype(jnp.float32)
        mid_low[head_z] = total.astype(jnp.bfloat16)

        @pl.when(head_z != col)
        def _(head_z=head_z):
            fin_copy(head_z, place_of(head_z)).start()

        @pl.when(head_z == col)
        def _(head_z=head_z):
            pltpu.make_async_copy(
                mid_low.at[head_z], fin_got.at[place_of(head_z)], fin_recv
            ).start()

    returns[2].wait_recv()
    returns[4].wait_recv()
    dk_out[...] = (
        dk_sum[0:keys, :] * scale + kv_got[2].astype(jnp.float32) + kv_got[4].astype(jnp.float32)
    )
    returns[3].wait_recv()
    returns[5].wait_recv()
    dv_out[...] = (
        dv_sum[0:keys, :] + kv_got[3].astype(jnp.float32) + kv_got[5].astype(jnp.float32)
    )
    for copy in biases:
        copy.wait()
    db_out[...] = db_own[0:1, 0:levels] + sum(db_got[n, 0:1, 0:levels] for n in range(7))

    pltpu.make_async_copy(fin_got, fin_got, fin_recv).wait()
    for head in range(4):
        dq_out[:, head * dim : (head + 1) * dim] = fin_got[head].astype(jnp.float32)

    def drain(buffer, sem, short):
        @pl.when(short)
        def _():
            part = buffer.at[pl.ds(0, queries - rows), :]
            pltpu.make_async_copy(part, part, sem).wait()

        @pl.when(jnp.logical_not(short))
        def _():
            pltpu.make_async_copy(buffer, buffer, sem).wait()

    drain(q_all, q_send, own_row)
    drain(g_all, g_send, own_row)
    drain(dq_all, dq_send, mid_self)
    for copy in gaps + sides + [k_pass, v_pass] + returns:
        copy.wait_send()
    for head_z in range(4):

        @pl.when(head_z != col)
        def _(head_z=head_z):
            fin_copy(head_z, place_of(head_z)).wait_send()


def place_kernel(dq, dk, dv, db, dq_out, dk_out, dv_out, db_out, sems):
    copies = [
        pltpu.make_async_copy(src, dst, sems.at[n])
        for n, (src, dst) in enumerate(((dq, dq_out), (dk, dk_out), (dv, dv_out), (db, db_out)))
    ]
    for copy in copies:
        copy.start()
    for copy in copies:
        copy.wait()


def per_device(queries_in, key_states, value_states, grad_output, bias_table, gap_bucket, order):
    vmem = pl.BlockSpec(memory_space=pltpu.VMEM)
    anywhere = pl.BlockSpec(memory_space=pl.ANY)
    low, full = jnp.bfloat16, jnp.float32
    dma = pltpu.SemaphoreType.DMA
    outs = (
        jax.ShapeDtypeStruct((rows, 4 * dim), full),
        jax.ShapeDtypeStruct((keys, dim), full),
        jax.ShapeDtypeStruct((keys, dim), full),
        jax.ShapeDtypeStruct((1, levels), full),
    )
    results = pl.pallas_call(
        kernel,
        out_shape=outs,
        in_specs=[
            anywhere,
            anywhere,
            anywhere,
            anywhere,
            vmem,
            vmem,
            pl.BlockSpec(memory_space=pltpu.SMEM),
        ],
        out_specs=(vmem, vmem, vmem, vmem),
        scratch_shapes=[
            pltpu.VMEM((queries, dim), low),
            pltpu.VMEM((queries, dim), low),
            pltpu.VMEM((blocks, keys, dim), low),
            pltpu.VMEM((blocks, keys, dim), low),
            pltpu.VMEM((tiles, dim, tile), low),
            pltpu.VMEM((blocks, 8, 640), full),
            pltpu.VMEM((all_keys, dim), full),
            pltpu.VMEM((all_keys, dim), full),
            pltpu.VMEM((all_keys, dim), jnp.int32),
            pltpu.VMEM((1, queries), jnp.int32),
            pltpu.VMEM((all_keys, queries), full),
            pltpu.VMEM((all_keys, queries), full),
            pltpu.VMEM((blocks, 8, queries), full),
            pltpu.VMEM((8, queries), full),
            pltpu.VMEM((8, queries), full),
            pltpu.VMEM((dim, chunk), full),
            pltpu.VMEM((queries, dim), low),
            pltpu.VMEM((4, 2 * rows, dim), low),
            pltpu.VMEM((4, rows, dim), low),
            pltpu.VMEM((4, rows, dim), low),
            pltpu.VMEM((all_keys, dim), full),
            pltpu.VMEM((all_keys, dim), full),
            pltpu.VMEM((all_keys, dim), full),
            pltpu.VMEM((6, keys, dim), low),
            pltpu.VMEM((6, keys, dim), low),
            pltpu.VMEM((8, dim), full),
            pltpu.VMEM((7, 8, dim), full),
            dma((2,)),
            dma((3,)),
            dma((3,)),
            dma((3,)),
            dma((3,)),
            dma((3,)),
            dma((3,)),
            dma(()),
            dma((4,)),
            dma(()),
            dma((4,)),
            dma((chunks,)),
            dma((chunks,)),
            dma(()),
            dma((4,)),
            dma((4,)),
            dma(()),
            dma((6,)),
            dma((6,)),
            dma((7,)),
            dma((7,)),
        ],
        compiler_params=pltpu.CompilerParams(
            collective_id=0, has_side_effects=True, vmem_limit_bytes=60 * 1024 * 1024
        ),
        cost_estimate=pl.CostEstimate(
            flops=10 * all_keys * queries * dim,
            bytes_accessed=8 * queries * dim,
            transcendentals=2 * all_keys * queries,
        ),
    )(
        queries_in,
        grad_output,
        key_states,
        value_states,
        bias_table,
        gap_bucket,
        order,
    )
    return pl.pallas_call(
        place_kernel,
        out_shape=outs,
        in_specs=[anywhere] * 4,
        out_specs=(anywhere,) * 4,
        scratch_shapes=[dma((4,))],
    )(*results)


def solution(mesh):
    placed = (
        P("row", None),
        P(("col", "depth"), "row"),
        P(("col", "depth"), "row"),
        P("row", None),
        P(),
        P(("col", "depth")),
        P(),
    )
    return jax.shard_map(
        per_device,
        mesh=mesh,
        in_specs=placed,
        out_specs=(
            P("row", ("col", "depth")),
            P(("col", "depth"), "row"),
            P(("col", "depth"), "row"),
            P("row", None),
        ),
        check_vma=False,
    )
```

```python
import functools
import math

import jax
import jax.numpy as jnp
from jax import lax
from jax.experimental import pallas as pl
from jax.experimental.pallas import tpu as pltpu
from jax.sharding import PartitionSpec as P

rows = 144
dim = 128
keys = 576
blocks = 4
all_keys = blocks * keys
levels = 64
slots = 8
queries = slots * rows
cuts = (0, 512, 1152)
chunks = len(cuts) - 1
z_steps = (0, 1, 3, 2)
scale = dim ** -0.5
log2e = math.log2(math.e)
masked_value = -1e30
floor_value = -1e20
MESH = pl.DeviceIdType.MESH


def fold(a, combine):
    return combine(a.reshape(a.shape[0] // 8, 8, a.shape[1]), axis=0)


def wide(a, count):
    return jnp.concatenate([a] * (count // dim), axis=1)


def nt_dot(a, b):
    return lax.dot_general(a, b, (((1,), (1,)), ((), ())), preferred_element_type=jnp.float32)


def nn_dot(a, b):
    return jnp.dot(a, b, preferred_element_type=jnp.float32)


def column_of(row):
    pieces = []
    eye = lax.broadcasted_iota(jnp.int32, (dim, dim), 0) == lax.broadcasted_iota(
        jnp.int32, (dim, dim), 1
    )
    for start in range(0, keys, dim):
        spread = jnp.broadcast_to(row[:, start : start + dim], (dim, dim))
        column = jnp.sum(jnp.where(eye, spread, 0.0), axis=1, keepdims=True)
        pieces.append(column[: min(dim, keys - start)])
    return jnp.concatenate(pieces, axis=0)


def merge(parts):
    best = functools.reduce(jnp.maximum, [a[0:1] for a in parts])
    factors = [jnp.exp2(a[0:1] - best) for a in parts]
    total = sum(a[1:2] * f for a, f in zip(parts, factors))
    moment = sum(a[2:3] * f for a, f in zip(parts, factors))
    return best, total, moment


def kernel(
    q_ref,
    g_ref,
    k_ref,
    v_ref,
    table_ref,
    gap_ref,
    order_ref,
    dq_out,
    dk_out,
    dv_out,
    db_out,
    q_all,
    g_all,
    k_all,
    v_all,
    k_turned,
    gap_rows,
    gap_cols,
    bias_cols,
    key_pos,
    query_pos,
    s_all,
    dp_all,
    state,
    stats,
    stats_got,
    dq_all,
    dq_got,
    dk_sum,
    dv_sum,
    ds_sum,
    kv_low,
    kv_got,
    db_own,
    db_got,
    local_sem,
    gap_send,
    gap_recv,
    k_send,
    k_recv,
    v_send,
    v_recv,
    q_send,
    q_recv,
    g_send,
    g_recv,
    st_send,
    st_recv,
    dq_send,
    dq_recv,
    dkv_send,
    dkv_recv,
    db_send,
    db_recv,
):
    row = lax.axis_index("row")
    col = lax.axis_index("col")
    depth = lax.axis_index("depth")
    z_lo = row // 8
    x = (row // 2) % 4
    core = row % 2
    z = depth * 4 + z_lo
    member = col // 2
    parity = col % 2
    other = (core + member) % 2
    own_row = col == 0
    mid_self = (col == 0) & (z_lo == 0) & (depth == x // 2)

    def shift(j):
        return (parity + (1 if j in (1, 2) else 0)) % 2

    def at(step, xx):
        there = (z + step + 8) % 8
        return ((there % 4) * 8 + xx * 2 + other, col, there // 4)

    def slot_x(s):
        return (x + shift(s // 2) + 2 * (s % 2)) % 4

    def peer(a, b):
        return (row, (col + a) % 4, (depth + b) % 2)

    barrier = pltpu.get_barrier_semaphore()

    def greet(device):
        pl.semaphore_signal(barrier, inc=1, device_id=device, device_id_type=MESH)

    for step, j in ((0, 0), (1, 1), (-1, 2), (2, 3), (-2, 3)):
        for i in range(2):
            device = at(step, (x + shift(j) + 2 * i) % 4)
            if step == 0 and i == 0:

                @pl.when(jnp.logical_not(own_row))
                def _(device=device):
                    greet(device)

            else:
                greet(device)
    for n in range(1, 8):
        greet(peer(n // 2, n % 2))
    for n in range(8):
        from_col, from_depth = n // 2, n % 2
        head_x = depth * 2 + (x + z_lo + 4 - col + from_col) % 2
        head_core = (core + from_col // 2) % 2

        @pl.when(jnp.logical_not(mid_self & (from_col == 0) & (depth == from_depth)))
        def _(device=(col * 8 + head_x * 2 + head_core, from_col, from_depth)):
            greet(device)

    own_k = pltpu.make_async_copy(k_ref, k_all.at[0], local_sem.at[0])
    own_v = pltpu.make_async_copy(v_ref, v_all.at[0], local_sem.at[1])
    own_k.start()
    own_v.start()
    gap_rows[0] = jnp.zeros((8, 640), jnp.float32)
    gap_rows[0, 0:1, 0:keys] = gap_ref[...].astype(jnp.float32).reshape(1, keys)

    pl.semaphore_wait(
        barrier, 25 - own_row.astype(jnp.int32) - mid_self.astype(jnp.int32)
    )

    def remote(src, dst, send_sem, recv_sem, device):
        return pltpu.make_async_remote_copy(
            src_ref=src,
            dst_ref=dst,
            send_sem=send_sem,
            recv_sem=recv_sem,
            device_id=device,
            device_id_type=MESH,
        )

    def gap_copy(a):
        return remote(
            gap_rows.at[0], gap_rows.at[4 - a], gap_send.at[a - 1], gap_recv.at[3 - a], peer(a, 0)
        )

    def own_copy(a, src, dst, send, recv):
        return remote(src, dst.at[4 - a], send.at[a - 1], recv.at[3 - a], peer(a, 0))

    def pass_copy(a, dst, send, recv):
        return remote(dst.at[4 - a], dst.at[2], send.at[1], recv.at[1], peer(a, 0))

    gaps = [gap_copy(a) for a in (1, 3, 2)]
    sides = [own_copy(a, k_ref, k_all, k_send, k_recv) for a in (1, 3)] + [
        own_copy(a, v_ref, v_all, v_send, v_recv) for a in (3, 1)
    ]
    k_pass = pass_copy(1, k_all, k_send, k_recv)
    v_pass = pass_copy(3, v_all, v_send, v_recv)
    for copy in (sides[0], sides[2]):
        copy.start()

    def send_rows(src, dst, send_sem, recv_sem, step, j):
        for i in range(2):
            target = at(step, (x + 3 * shift(j) + 2 * i) % 4)
            src_part = src.at[:, pl.ds(pl.multiple_of(target[0] * dim, dim), dim)]
            dst_part = dst.at[pl.ds((j * 2 + i) * rows, rows), :]
            away = remote(src_part, dst_part, send_sem, recv_sem.at[j], target)
            if step == 0 and i == 0:

                @pl.when(own_row)
                def _(src_part=src_part, dst_part=dst_part):
                    pltpu.make_async_copy(src_part, dst_part, recv_sem.at[j]).start()

                @pl.when(jnp.logical_not(own_row))
                def _(away=away):
                    away.start()

            else:
                away.start()

    send_rows(q_ref, q_all, q_send, q_recv, 0, 0)
    send_rows(g_ref, g_all, g_send, g_recv, 0, 0)
    for copy in gaps:
        copy.start()
    send_rows(q_ref, q_all, q_send, q_recv, -1, 1)
    send_rows(q_ref, q_all, q_send, q_recv, 1, 2)
    send_rows(q_ref, q_all, q_send, q_recv, -2, 3)
    send_rows(g_ref, g_all, g_send, g_recv, -1, 1)
    send_rows(g_ref, g_all, g_send, g_recv, 1, 2)
    send_rows(g_ref, g_all, g_send, g_recv, 2, 3)
    for copy in (sides[1], sides[3]):
        copy.start()

    lane = lax.broadcasted_iota(jnp.int32, (1, queries), 1)
    half = rows // 2
    pos = jnp.zeros((1, queries), jnp.int32)
    for s in range(slots):
        r = ((z_lo + z_steps[s // 2]) % 4) * 8 + slot_x(s) * 2 + other
        for b in range(2):
            low = s * rows + b * half
            inside = (lane >= low) & (lane < low + half)
            pos = jnp.where(inside, order_ref[2 * r + b] * half + lane - low, pos)
    query_pos[...] = pos
    within = lax.broadcasted_iota(jnp.int32, (keys, dim), 0)
    for b in range(blocks):
        key_pos[b * keys : (b + 1) * keys, :] = within + (((col + b) % 4) * 2 + depth) * keys
    level = lax.broadcasted_iota(jnp.int32, (1, levels), 1).astype(jnp.float32)
    table = table_ref[pl.ds(row, 1), :]

    def fill_bias(b):
        start = b * keys
        column = column_of(gap_rows[b, 0:1, :])
        gap_cols[start : start + keys, :] = jnp.broadcast_to(column, (keys, dim))
        bias = jnp.sum(jnp.where(column == level, table, 0.0), axis=1, keepdims=True)
        bias_cols[start : start + keys, :] = jnp.broadcast_to(bias * log2e, (keys, dim))

    def turn(b):
        k_turned[b] = k_all[b].astype(jnp.float32).T.astype(jnp.bfloat16)

    fill_bias(0)
    fresh = jnp.zeros((8, queries), jnp.float32)
    state[0] = fresh + floor_value
    state[1] = fresh
    state[2] = fresh
    own_k.wait()
    own_v.wait()
    turn(0)

    sides[0].wait_recv()
    k_pass.start()
    sides[2].wait_recv()
    v_pass.start()

    def wait_group(buffer, sem, j):
        part = buffer.at[pl.ds(j * 2 * rows, 2 * rows), :]
        pltpu.make_async_copy(part, part, sem.at[j]).wait()

    def first_pass(c, b):
        lo, hi = cuts[c], cuts[c + 1]
        count = hi - lo
        part = slice(b * keys, (b + 1) * keys)
        s = nt_dot(k_all[b], q_all[lo:hi, :]) * (scale * log2e)
        s = s + wide(bias_cols[part, :], count)
        s = jnp.where(wide(key_pos[part, :], count) <= query_pos[:, lo:hi], s, masked_value)
        s_all[part, lo:hi] = s
        dp = nt_dot(v_all[b], g_all[lo:hi, :])
        dp_all[part, lo:hi] = dp
        before = state[0, :, lo:hi]
        best = jnp.maximum(before, fold(s, jnp.max))
        factor = jnp.exp2(before - best)
        w = jnp.exp2(s.reshape(keys // 8, 8, count) - best[None])
        wd = w * dp.reshape(keys // 8, 8, count)
        state[0, :, lo:hi] = best
        state[1, :, lo:hi] = state[1, :, lo:hi] * factor + jnp.sum(w, axis=0)
        state[2, :, lo:hi] = state[2, :, lo:hi] * factor + jnp.sum(wd, axis=0)

    def stat_copy(c):
        part = pl.ds(cuts[c], cuts[c + 1] - cuts[c])
        return remote(
            stats.at[:, part], stats_got.at[:, part], st_send.at[c], st_recv.at[c], peer(0, 1)
        )

    def close(c):
        lo, hi = cuts[c], cuts[c + 1]
        best = jnp.max(state[0, :, lo:hi], axis=0, keepdims=True)
        factor = jnp.exp2(state[0, :, lo:hi] - best)
        stats[0:1, lo:hi] = best
        stats[1:2, lo:hi] = jnp.sum(state[1, :, lo:hi] * factor, axis=0, keepdims=True)
        stats[2:3, lo:hi] = jnp.sum(state[2, :, lo:hi] * factor, axis=0, keepdims=True)
        stat_copy(c).start()

    wait_group(q_all, q_recv, 0)
    wait_group(g_all, g_recv, 0)
    wait_group(q_all, q_recv, 1)
    wait_group(g_all, g_recv, 1)
    first_pass(0, 0)
    for copy in gaps:
        copy.wait_recv()
    for b in (3, 1, 2):
        fill_bias(b)
    sides[1].wait_recv()
    sides[3].wait_recv()
    turn(1)
    turn(3)
    first_pass(0, 1)
    first_pass(0, 3)
    for j in (2, 3):
        wait_group(q_all, q_recv, j)
        wait_group(g_all, g_recv, j)
    for b in (0, 1, 3):
        first_pass(1, b)
    k_pass.wait_recv()
    v_pass.wait_recv()
    for c in range(chunks):
        first_pass(c, 2)
        close(c)
    turn(2)

    def kv_copy(n, a):
        return remote(
            kv_low.at[n], kv_got.at[n], dkv_send.at[n], dkv_recv.at[n], peer(a, 0)
        )

    returns = [kv_copy(n, a) for n, a in enumerate((1, 3, 3, 1, 1, 3))]

    def low(total, b, factor):
        return (total[b * keys : (b + 1) * keys, :] * factor).astype(jnp.bfloat16)

    sent = 0
    for c in range(chunks):
        lo, hi = cuts[c], cuts[c + 1]
        stat_copy(c).wait()
        best, total, moment = merge([stats[0:3, lo:hi], stats_got[0:3, lo:hi]])
        lse = best + jnp.log(total) * log2e
        delta = moment / total

        def grads(b):
            part = slice(b * keys, (b + 1) * keys)
            p = jnp.exp2(s_all[part, lo:hi] - lse)
            ds = p * (dp_all[part, lo:hi] - delta)
            ds_lanes = sum(ds[:, n * dim : (n + 1) * dim] for n in range((hi - lo) // dim))
            ds_low = ds.astype(jnp.bfloat16)
            dv_part = nn_dot(p.astype(jnp.bfloat16), g_all[lo:hi, :])
            dk_part = nn_dot(ds_low, q_all[lo:hi, :])
            if c == 0:
                ds_sum[part, :] = ds_lanes
                dv_sum[part, :] = dv_part
                dk_sum[part, :] = dk_part
            else:
                ds_sum[part, :] += ds_lanes
                dv_sum[part, :] += dv_part
                dk_sum[part, :] += dk_part
            return nn_dot(k_turned[b], ds_low)

        dq = grads(2) + grads(3)
        if c == chunks - 1:
            kv_low[0] = low(dk_sum, 2, scale)
            returns[0].start()
            kv_low[1] = low(dv_sum, 2, 1.0)
            returns[1].start()
            kv_low[2] = low(dk_sum, 3, scale)
            returns[2].start()
        dq = dq + (grads(1) + grads(0))
        if c == chunks - 1:
            kv_low[3] = low(dv_sum, 1, 1.0)
            returns[3].start()
        dq_all[lo:hi, :] = (dq.T * scale).astype(jnp.bfloat16)
        while (sent + 1) * rows <= hi:
            j = sent // 2
            src = dq_all.at[pl.ds(sent * rows, rows), :]
            place = (x % 2) * 2 + core
            dst = dq_got.at[place, pl.ds(pl.multiple_of(depth * rows, rows), rows), :]
            target = (((z_lo + z_steps[j]) % 4) * 8 + slot_x(sent) * 2 + other, z_lo, x // 2)
            away = remote(src, dst, dq_send, dq_recv.at[place], target)
            if sent == 0:

                @pl.when(mid_self)
                def _(src=src, dst=dst, place=place):
                    pltpu.make_async_copy(src, dst, dq_recv.at[place]).start()

                @pl.when(jnp.logical_not(mid_self))
                def _(away=away):
                    away.start()

            else:
                away.start()
            sent += 1

    column = jnp.sum(ds_sum[...], axis=1, keepdims=True)
    by_level = jnp.where(gap_cols[:, 0:levels] == level, column, 0.0)
    db_own[...] = jnp.zeros_like(db_own)
    db_own[0:1, 0:levels] = jnp.sum(by_level, axis=0, keepdims=True)
    biases = [
        remote(db_own, db_got.at[n - 1], db_send.at[n - 1], db_recv.at[n - 1], peer(n // 2, n % 2))
        for n in range(1, 8)
    ]
    for copy in biases:
        copy.start()

    returns[0].wait_recv()
    kv_low[4] = (dk_sum[keys : 2 * keys, :] * scale + kv_got[0].astype(jnp.float32)).astype(
        jnp.bfloat16
    )
    returns[4].start()
    returns[1].wait_recv()
    kv_low[5] = (dv_sum[3 * keys : 4 * keys, :] + kv_got[1].astype(jnp.float32)).astype(
        jnp.bfloat16
    )
    returns[5].start()

    returns[2].wait_recv()
    returns[4].wait_recv()
    dk_out[...] = (
        dk_sum[0:keys, :] * scale + kv_got[2].astype(jnp.float32) + kv_got[4].astype(jnp.float32)
    )
    returns[3].wait_recv()
    returns[5].wait_recv()
    dv_out[...] = (
        dv_sum[0:keys, :] + kv_got[3].astype(jnp.float32) + kv_got[5].astype(jnp.float32)
    )
    for copy in biases:
        copy.wait()
    db_out[...] = db_own[0:1, 0:levels] + sum(db_got[n, 0:1, 0:levels] for n in range(7))

    for head in range(4):
        both = dq_got.at[head]
        pltpu.make_async_copy(both, both, dq_recv.at[head]).wait()
        dq_out[:, head * dim : (head + 1) * dim] = both[0:rows, :].astype(jnp.float32) + both[
            rows : 2 * rows, :
        ].astype(jnp.float32)

    def drain(buffer, sem, short):
        @pl.when(short)
        def _():
            part = buffer.at[pl.ds(0, queries - rows), :]
            pltpu.make_async_copy(part, part, sem).wait()

        @pl.when(jnp.logical_not(short))
        def _():
            pltpu.make_async_copy(buffer, buffer, sem).wait()

    drain(q_all, q_send, own_row)
    drain(g_all, g_send, own_row)
    drain(dq_all, dq_send, mid_self)
    for copy in gaps + sides + [k_pass, v_pass] + returns:
        copy.wait_send()


def place_kernel(dq, dk, dv, db, dq_out, dk_out, dv_out, db_out):
    dq_out[...] = dq[...]
    dk_out[...] = dk[...]
    dv_out[...] = dv[...]
    db_out[...] = db[...]


def per_device(queries_in, key_states, value_states, grad_output, bias_table, gap_bucket, order):
    vmem = pl.BlockSpec(memory_space=pltpu.VMEM)
    hbm = pl.BlockSpec(memory_space=pltpu.HBM)
    low, full = jnp.bfloat16, jnp.float32
    dma = pltpu.SemaphoreType.DMA
    outs = (
        jax.ShapeDtypeStruct((rows, 4 * dim), full),
        jax.ShapeDtypeStruct((keys, dim), full),
        jax.ShapeDtypeStruct((keys, dim), full),
        jax.ShapeDtypeStruct((1, levels), full),
    )
    results = pl.pallas_call(
        kernel,
        out_shape=outs,
        in_specs=[
            hbm,
            hbm,
            hbm,
            hbm,
            vmem,
            vmem,
            pl.BlockSpec(memory_space=pltpu.SMEM),
        ],
        out_specs=(vmem, vmem, vmem, vmem),
        scratch_shapes=[
            pltpu.VMEM((queries, dim), low),
            pltpu.VMEM((queries, dim), low),
            pltpu.VMEM((blocks, keys, dim), low),
            pltpu.VMEM((blocks, keys, dim), low),
            pltpu.VMEM((blocks, dim, keys), low),
            pltpu.VMEM((blocks, 8, 640), full),
            pltpu.VMEM((all_keys, dim), full),
            pltpu.VMEM((all_keys, dim), full),
            pltpu.VMEM((all_keys, dim), jnp.int32),
            pltpu.VMEM((1, queries), jnp.int32),
            pltpu.VMEM((all_keys, queries), full),
            pltpu.VMEM((all_keys, queries), full),
            pltpu.VMEM((3, 8, queries), full),
            pltpu.VMEM((8, queries), full),
            pltpu.VMEM((8, queries), full),
            pltpu.VMEM((queries, dim), low),
            pltpu.VMEM((4, 2 * rows, dim), low),
            pltpu.VMEM((all_keys, dim), full),
            pltpu.VMEM((all_keys, dim), full),
            pltpu.VMEM((all_keys, dim), full),
            pltpu.VMEM((6, keys, dim), low),
            pltpu.VMEM((6, keys, dim), low),
            pltpu.VMEM((8, dim), full),
            pltpu.VMEM((7, 8, dim), full),
            dma((2,)),
            dma((3,)),
            dma((3,)),
            dma((3,)),
            dma((3,)),
            dma((3,)),
            dma((3,)),
            dma(()),
            dma((4,)),
            dma(()),
            dma((4,)),
            dma((chunks,)),
            dma((chunks,)),
            dma(()),
            dma((4,)),
            dma((6,)),
            dma((6,)),
            dma((7,)),
            dma((7,)),
        ],
        compiler_params=pltpu.CompilerParams(
            collective_id=0, has_side_effects=True, vmem_limit_bytes=60 * 1024 * 1024
        ),
        cost_estimate=pl.CostEstimate(
            flops=10 * all_keys * queries * dim,
            bytes_accessed=8 * queries * dim,
            transcendentals=2 * all_keys * queries,
        ),
    )(
        queries_in,
        grad_output,
        key_states,
        value_states,
        bias_table,
        gap_bucket,
        order,
    )
    return pl.pallas_call(
        place_kernel,
        out_shape=outs,
        in_specs=[vmem] * 4,
        out_specs=(vmem,) * 4,
    )(*results)


def solution(mesh):
    placed = (
        P("row", None),
        P(("col", "depth"), "row"),
        P(("col", "depth"), "row"),
        P("row", None),
        P(),
        P(("col", "depth")),
        P(),
    )
    return jax.shard_map(
        per_device,
        mesh=mesh,
        in_specs=placed,
        out_specs=(
            P("row", ("col", "depth")),
            P(("col", "depth"), "row"),
            P(("col", "depth"), "row"),
            P("row", None),
        ),
        check_vma=False,
    )
```

```python
import functools
import math

import jax
import jax.numpy as jnp
from jax import lax
from jax.experimental import pallas as pl
from jax.experimental.pallas import tpu as pltpu
from jax.sharding import PartitionSpec as P

rows = 144
dim = 128
keys = 576
half_keys = keys // 2
blocks = 4
all_keys = blocks * keys
levels = 64
slots = 8
queries = slots * rows
cuts = (0, 512, 1152)
chunks = len(cuts) - 1
z_steps = (0, 1, 3, 2)
scale = dim ** -0.5
log2e = math.log2(math.e)
masked_value = -1e30
floor_value = -1e20
MESH = pl.DeviceIdType.MESH


def fold(a, combine):
    return combine(a.reshape(a.shape[0] // 8, 8, a.shape[1]), axis=0)


def wide(a, count):
    return jnp.concatenate([a] * (count // dim), axis=1)


def nt_dot(a, b):
    return lax.dot_general(a, b, (((1,), (1,)), ((), ())), preferred_element_type=jnp.float32)


def nn_dot(a, b):
    return jnp.dot(a, b, preferred_element_type=jnp.float32)


def column_of(row):
    pieces = []
    eye = lax.broadcasted_iota(jnp.int32, (dim, dim), 0) == lax.broadcasted_iota(
        jnp.int32, (dim, dim), 1
    )
    for start in range(0, keys, dim):
        spread = jnp.broadcast_to(row[:, start : start + dim], (dim, dim))
        column = jnp.sum(jnp.where(eye, spread, 0.0), axis=1, keepdims=True)
        pieces.append(column[: min(dim, keys - start)])
    return jnp.concatenate(pieces, axis=0)


def merge(parts):
    best = functools.reduce(jnp.maximum, [a[0:1] for a in parts])
    factors = [jnp.exp2(a[0:1] - best) for a in parts]
    total = sum(a[1:2] * f for a, f in zip(parts, factors))
    moment = sum(a[2:3] * f for a, f in zip(parts, factors))
    return best, total, moment


def kernel(
    q_ref,
    g_ref,
    k_ref,
    v_ref,
    table_hbm,
    gap_hbm,
    order_hbm,
    dq_hbm,
    dk_hbm,
    dv_hbm,
    db_hbm,
    dq_out,
    dk_out,
    dv_out,
    db_out,
    table_ref,
    gap_ref,
    order_ref,
    q_all,
    g_all,
    k_all,
    v_all,
    k_turned,
    gap_rows,
    gap_cols,
    bias_cols,
    key_pos,
    query_pos,
    s_all,
    dp_all,
    state,
    stats,
    stats_got,
    dq_all,
    dq_got,
    dk_sum,
    dv_sum,
    ds_sum,
    kv_low,
    kv_got,
    db_own,
    db_got,
    local_sem,
    store_sem,
    gap_send,
    gap_recv,
    k_send,
    k_recv,
    v_send,
    v_recv,
    q_send,
    q_recv,
    g_send,
    g_recv,
    st_send,
    st_recv,
    dq_send,
    dq_recv,
    dkv_send,
    dkv_recv,
    db_send,
    db_recv,
):
    row = lax.axis_index("row")
    col = lax.axis_index("col")
    depth = lax.axis_index("depth")
    z_lo = row // 8
    x = (row // 2) % 4
    core = row % 2
    z = depth * 4 + z_lo
    member = col // 2
    parity = col % 2
    other = (core + member) % 2
    own_row = col == 0
    mid_self = (col == 0) & (z_lo == 0) & (depth == x // 2)

    def shift(j):
        return (parity + (1 if j in (1, 2) else 0)) % 2

    def at(step, xx):
        there = (z + step + 8) % 8
        return ((there % 4) * 8 + xx * 2 + other, col, there // 4)

    def slot_x(s):
        return (x + shift(s // 2) + 2 * (s % 2)) % 4

    def peer(a, b):
        return (row, (col + a) % 4, (depth + b) % 2)

    loads = [
        pltpu.make_async_copy(src, dst, local_sem.at[n])
        for n, (src, dst) in enumerate(
            (
                (k_ref, k_all.at[0]),
                (v_ref, v_all.at[0]),
                (gap_hbm, gap_ref),
                (table_hbm, table_ref),
                (order_hbm, order_ref),
            )
        )
    ]
    for copy in loads:
        copy.start()

    barrier = pltpu.get_barrier_semaphore()

    def greet(device):
        pl.semaphore_signal(barrier, inc=1, device_id=device, device_id_type=MESH)

    for n in range(8):
        from_col, from_depth = n // 2, n % 2
        head_x = depth * 2 + (x + z_lo + 4 - col + from_col) % 2
        head_core = (core + from_col // 2) % 2

        @pl.when(jnp.logical_not(mid_self & (from_col == 0) & (depth == from_depth)))
        def _(device=(col * 8 + head_x * 2 + head_core, from_col, from_depth)):
            greet(device)

    for n in (5, 7, 3, 4, 1, 6, 2):
        greet(peer(n // 2, n % 2))
    for step, j in ((2, 3), (-2, 3), (1, 1), (-1, 2), (0, 0)):
        for i in range(2):
            device = at(step, (x + shift(j) + 2 * i) % 4)
            if step == 0 and i == 0:

                @pl.when(jnp.logical_not(own_row))
                def _(device=device):
                    greet(device)

            else:
                greet(device)
    loads[2].wait()
    gap_rows[0] = jnp.zeros((1, 640), jnp.float32)
    gap_rows[0, 0:1, 0:keys] = gap_ref[...].astype(jnp.float32).reshape(1, keys)

    pl.semaphore_wait(
        barrier,
        25 - own_row.astype(jnp.int32) - mid_self.astype(jnp.int32),
    )

    def remote(src, dst, send_sem, recv_sem, device):
        return pltpu.make_async_remote_copy(
            src_ref=src,
            dst_ref=dst,
            send_sem=send_sem,
            recv_sem=recv_sem,
            device_id=device,
            device_id_type=MESH,
        )

    def gap_copy(a):
        return remote(
            gap_rows.at[0], gap_rows.at[4 - a], gap_send.at[a - 1], gap_recv.at[3 - a], peer(a, 0)
        )

    def own_copy(a, h, src, dst, send, recv):
        part = pl.ds(h * half_keys, half_keys)
        return remote(
            src.at[part, :],
            dst.at[4 - a, part, :],
            send.at[a - 1, h],
            recv.at[3 - a, h],
            peer(a, 0),
        )

    def pass_copy(a, h, dst, send, recv):
        part = pl.ds(h * half_keys, half_keys)
        return remote(
            dst.at[4 - a, part, :], dst.at[2, part, :], send.at[1, h], recv.at[1, h], peer(a, 0)
        )

    gaps = [gap_copy(a) for a in (1, 3, 2)]
    passed, direct, onward = [], [], []
    for h in range(2):
        passed.append(own_copy(1, h, k_ref, k_all, k_send, k_recv))
        passed.append(own_copy(3, h, v_ref, v_all, v_send, v_recv))
        direct.append(own_copy(3, h, k_ref, k_all, k_send, k_recv))
        direct.append(own_copy(1, h, v_ref, v_all, v_send, v_recv))
        onward.append(pass_copy(1, h, k_all, k_send, k_recv))
        onward.append(pass_copy(3, h, v_all, v_send, v_recv))
    for copy in passed:
        copy.start()

    def send_rows(src, dst, send_sem, recv_sem, step, j):
        for i in range(2):
            target = at(step, (x + 3 * shift(j) + 2 * i) % 4)
            src_part = src.at[:, pl.ds(pl.multiple_of(target[0] * dim, dim), dim)]
            dst_part = dst.at[pl.ds((j * 2 + i) * rows, rows), :]
            away = remote(src_part, dst_part, send_sem, recv_sem.at[j], target)
            if step == 0 and i == 0:

                @pl.when(own_row)
                def _(src_part=src_part, dst_part=dst_part):
                    pltpu.make_async_copy(src_part, dst_part, recv_sem.at[j]).start()

                @pl.when(jnp.logical_not(own_row))
                def _(away=away):
                    away.start()

            else:
                away.start()

    send_rows(q_ref, q_all, q_send, q_recv, 0, 0)
    send_rows(g_ref, g_all, g_send, g_recv, 0, 0)
    for copy in gaps:
        copy.start()
    send_rows(q_ref, q_all, q_send, q_recv, -1, 1)
    send_rows(q_ref, q_all, q_send, q_recv, 1, 2)
    send_rows(q_ref, q_all, q_send, q_recv, -2, 3)
    send_rows(g_ref, g_all, g_send, g_recv, -1, 1)
    send_rows(g_ref, g_all, g_send, g_recv, 1, 2)
    send_rows(g_ref, g_all, g_send, g_recv, 2, 3)
    for copy in direct:
        copy.start()

    for n in (0, 1, 3, 4):
        loads[n].wait()

    lane = lax.broadcasted_iota(jnp.int32, (1, queries), 1)
    half = rows // 2
    pos = jnp.zeros((1, queries), jnp.int32)
    for s in range(slots):
        r = ((z_lo + z_steps[s // 2]) % 4) * 8 + slot_x(s) * 2 + other
        for b in range(2):
            low = s * rows + b * half
            inside = (lane >= low) & (lane < low + half)
            pos = jnp.where(inside, order_ref[2 * r + b] * half + lane - low, pos)
    query_pos[...] = pos
    within = lax.broadcasted_iota(jnp.int32, (keys, dim), 0)
    for b in range(blocks):
        key_pos[b * keys : (b + 1) * keys, :] = within + (((col + b) % 4) * 2 + depth) * keys
    level = lax.broadcasted_iota(jnp.int32, (1, levels), 1).astype(jnp.float32)
    table = table_ref[pl.ds(row, 1), :]

    def fill_bias(b):
        start = b * keys
        column = column_of(gap_rows[b, 0:1, :])
        gap_cols[start : start + keys, :] = jnp.broadcast_to(column, (keys, dim))
        bias = jnp.sum(jnp.where(column == level, table, 0.0), axis=1, keepdims=True)
        bias_cols[start : start + keys, :] = jnp.broadcast_to(bias * log2e, (keys, dim))

    def turn(b):
        k_turned[b] = k_all[b].astype(jnp.float32).T.astype(jnp.bfloat16)

    fill_bias(0)
    fresh = jnp.zeros((8, queries), jnp.float32)
    state[0] = fresh + floor_value
    state[1] = fresh
    state[2] = fresh
    turn(0)

    for come, go in zip(passed, onward):
        come.wait_recv()
        go.start()

    def wait_group(buffer, sem, j):
        part = buffer.at[pl.ds(j * 2 * rows, 2 * rows), :]
        pltpu.make_async_copy(part, part, sem.at[j]).wait()

    def first_pass(c, b):
        lo, hi = cuts[c], cuts[c + 1]
        count = hi - lo
        part = slice(b * keys, (b + 1) * keys)
        s = nt_dot(k_all[b], q_all[lo:hi, :]) * (scale * log2e)
        s = s + wide(bias_cols[part, :], count)
        s = jnp.where(wide(key_pos[part, :], count) <= query_pos[:, lo:hi], s, masked_value)
        s_all[part, lo:hi] = s
        dp = nt_dot(v_all[b], g_all[lo:hi, :])
        dp_all[part, lo:hi] = dp
        before = state[0, :, lo:hi]
        best = jnp.maximum(before, fold(s, jnp.max))
        factor = jnp.exp2(before - best)
        w = jnp.exp2(s.reshape(keys // 8, 8, count) - best[None])
        wd = w * dp.reshape(keys // 8, 8, count)
        state[0, :, lo:hi] = best
        state[1, :, lo:hi] = state[1, :, lo:hi] * factor + jnp.sum(w, axis=0)
        state[2, :, lo:hi] = state[2, :, lo:hi] * factor + jnp.sum(wd, axis=0)

    def stat_copy(c):
        part = pl.ds(cuts[c], cuts[c + 1] - cuts[c])
        return remote(
            stats.at[:, part], stats_got.at[:, part], st_send.at[c], st_recv.at[c], peer(0, 1)
        )

    def close(c):
        lo, hi = cuts[c], cuts[c + 1]
        best = jnp.max(state[0, :, lo:hi], axis=0, keepdims=True)
        factor = jnp.exp2(state[0, :, lo:hi] - best)
        stats[0:1, lo:hi] = best
        stats[1:2, lo:hi] = jnp.sum(state[1, :, lo:hi] * factor, axis=0, keepdims=True)
        stats[2:3, lo:hi] = jnp.sum(state[2, :, lo:hi] * factor, axis=0, keepdims=True)
        stat_copy(c).start()

    wait_group(q_all, q_recv, 0)
    wait_group(g_all, g_recv, 0)
    wait_group(q_all, q_recv, 1)
    wait_group(g_all, g_recv, 1)
    first_pass(0, 0)
    for copy in gaps:
        copy.wait_recv()
    for b in (3, 1, 2):
        fill_bias(b)
    for copy in direct:
        copy.wait_recv()
    turn(1)
    turn(3)
    first_pass(0, 1)
    first_pass(0, 3)
    for j in (2, 3):
        wait_group(q_all, q_recv, j)
        wait_group(g_all, g_recv, j)
    for b in (0, 1, 3):
        first_pass(1, b)
    for copy in onward:
        copy.wait_recv()
    for c in range(chunks):
        first_pass(c, 2)
        close(c)
    turn(2)

    def kv_copy(n, a):
        return remote(
            kv_low.at[n], kv_got.at[n], dkv_send.at[n], dkv_recv.at[n], peer(a, 0)
        )

    returns = [kv_copy(n, a) for n, a in enumerate((1, 3, 3, 1, 1, 3))]

    def low(total, b, factor):
        return (total[b * keys : (b + 1) * keys, :] * factor).astype(jnp.bfloat16)

    def dq_place(head_x, s):
        place = (head_x % 2) * 2 + core
        dst = dq_got.at[place, pl.ds(pl.multiple_of(depth * rows, rows), rows), :]
        there = (head_x + shift(s // 2) + 2 * (s % 2)) % 4
        target = (((z_lo + z_steps[s // 2]) % 4) * 8 + there * 2 + other, z_lo, head_x // 2)
        return dst, dq_recv.at[place], target

    def factors(c):
        lo, hi = cuts[c], cuts[c + 1]
        stat_copy(c).wait()
        best, total, moment = merge([stats[0:3, lo:hi], stats_got[0:3, lo:hi]])
        return best + jnp.log(total) * log2e, moment / total

    def grads(c, b, lse, delta):
        lo, hi = cuts[c], cuts[c + 1]
        part = slice(b * keys, (b + 1) * keys)
        p = jnp.exp2(s_all[part, lo:hi] - lse)
        ds = p * (dp_all[part, lo:hi] - delta)
        ds_lanes = sum(ds[:, n * dim : (n + 1) * dim] for n in range((hi - lo) // dim))
        ds_low = ds.astype(jnp.bfloat16)
        dv_part = nn_dot(p.astype(jnp.bfloat16), g_all[lo:hi, :])
        dk_part = nn_dot(ds_low, q_all[lo:hi, :])
        if c == 0:
            ds_sum[part, :] = ds_lanes
            dv_sum[part, :] = dv_part
            dk_sum[part, :] = dk_part
        else:
            ds_sum[part, :] += ds_lanes
            dv_sum[part, :] += dv_part
            dk_sum[part, :] += dk_part
        return nn_dot(k_turned[b], ds_low)

    def send_dq(c, dq):
        dq_all[cuts[c] : cuts[c + 1], :] = (dq.T * scale).astype(jnp.bfloat16)
        for s in range(cuts[c] // rows, cuts[c + 1] // rows):
            src = dq_all.at[pl.ds(s * rows, rows), :]
            dst, recv, target = dq_place(x, s)
            away = remote(src, dst, dq_send, recv, target)
            if s == 0:

                @pl.when(mid_self)
                def _(src=src, dst=dst, recv=recv):
                    pltpu.make_async_copy(src, dst, recv).start()

                @pl.when(jnp.logical_not(mid_self))
                def _(away=away):
                    away.start()

            else:
                away.start()

    def send_kv(n, total, b, factor):
        kv_low[n] = low(total, b, factor)
        returns[n].start()

    lse, delta = factors(0)
    send_dq(0, sum(grads(0, b, lse, delta) for b in (2, 3, 1, 0)))
    lse, delta = factors(1)
    dq = grads(1, 2, lse, delta)
    send_kv(0, dk_sum, 2, scale)
    send_kv(1, dv_sum, 2, 1.0)
    dq = dq + grads(1, 3, lse, delta)
    send_kv(2, dk_sum, 3, scale)
    dq = dq + grads(1, 1, lse, delta)
    send_kv(3, dv_sum, 1, 1.0)
    send_dq(1, dq + grads(1, 0, lse, delta))

    column = jnp.sum(ds_sum[...], axis=1, keepdims=True)
    by_level = jnp.where(gap_cols[:, 0:levels] == level, column, 0.0)
    db_own[...] = jnp.zeros_like(db_own)
    db_own[0:1, 0:levels] = jnp.sum(by_level, axis=0, keepdims=True)
    biases = [
        remote(db_own, db_got.at[n - 1], db_send.at[n - 1], db_recv.at[n - 1], peer(n // 2, n % 2))
        for n in range(1, 8)
    ]
    for copy in biases:
        copy.start()

    returns[0].wait_recv()
    kv_low[4] = (dk_sum[keys : 2 * keys, :] * scale + kv_got[0].astype(jnp.float32)).astype(
        jnp.bfloat16
    )
    returns[4].start()
    returns[1].wait_recv()
    kv_low[5] = (dv_sum[3 * keys : 4 * keys, :] + kv_got[1].astype(jnp.float32)).astype(
        jnp.bfloat16
    )
    returns[5].start()

    stores = [
        pltpu.make_async_copy(src, dst, store_sem.at[n])
        for n, (src, dst) in enumerate(((dk_out, dk_hbm), (dv_out, dv_hbm), (db_out, db_hbm)))
    ]
    returns[2].wait_recv()
    returns[4].wait_recv()
    dk_out[...] = (
        dk_sum[0:keys, :] * scale + kv_got[2].astype(jnp.float32) + kv_got[4].astype(jnp.float32)
    )
    stores[0].start()
    returns[3].wait_recv()
    returns[5].wait_recv()
    dv_out[...] = (
        dv_sum[0:keys, :] + kv_got[3].astype(jnp.float32) + kv_got[5].astype(jnp.float32)
    )
    stores[1].start()
    for copy in biases:
        copy.wait()
    db_out[...] = db_own[0:1, 0:levels] + sum(db_got[n, 0:1, 0:levels] for n in range(7))
    stores[2].start()

    for head in range(4):
        both = dq_got.at[head]
        pltpu.make_async_copy(both, both, dq_recv.at[head]).wait()
        dq_out[:, head * dim : (head + 1) * dim] = both[0:rows, :].astype(jnp.float32) + both[
            rows : 2 * rows, :
        ].astype(jnp.float32)
        part = pl.ds(head * dim, dim)
        stores.append(
            pltpu.make_async_copy(dq_out.at[:, part], dq_hbm.at[:, part], store_sem.at[3 + head])
        )
        stores[3 + head].start()

    def drain(buffer, sem, short):
        @pl.when(short)
        def _():
            part = buffer.at[pl.ds(0, queries - rows), :]
            pltpu.make_async_copy(part, part, sem).wait()

        @pl.when(jnp.logical_not(short))
        def _():
            pltpu.make_async_copy(buffer, buffer, sem).wait()

    drain(q_all, q_send, own_row)
    drain(g_all, g_send, own_row)
    drain(dq_all, dq_send, mid_self)

    for copy in stores:
        copy.wait()
    for copy in gaps + passed + direct + onward + returns:
        copy.wait_send()


def place_kernel(dq, dk, dv, db, dq_out, dk_out, dv_out, db_out):
    dq_out[...] = dq[...]
    dk_out[...] = dk[...]
    dv_out[...] = dv[...]
    db_out[...] = db[...]


def per_device(queries_in, key_states, value_states, grad_output, bias_table, gap_bucket, order):
    vmem = pl.BlockSpec(memory_space=pltpu.VMEM)
    hbm = pl.BlockSpec(memory_space=pltpu.HBM)
    low, full = jnp.bfloat16, jnp.float32
    dma = pltpu.SemaphoreType.DMA
    outs = (
        jax.ShapeDtypeStruct((rows, 4 * dim), full),
        jax.ShapeDtypeStruct((keys, dim), full),
        jax.ShapeDtypeStruct((keys, dim), full),
        jax.ShapeDtypeStruct((1, levels), full),
    )
    results = pl.pallas_call(
        kernel,
        out_shape=outs,
        in_specs=[
            hbm,
            hbm,
            hbm,
            hbm,
            hbm,
            hbm,
            hbm,
        ],
        out_specs=(hbm, hbm, hbm, hbm),
        scratch_shapes=[pltpu.VMEM(a.shape, full) for a in outs]
        + [
            pltpu.VMEM((32, levels), full),
            pltpu.VMEM((keys,), jnp.int32),
            pltpu.SMEM((64,), jnp.int32),
            pltpu.VMEM((queries, dim), low),
            pltpu.VMEM((queries, dim), low),
            pltpu.VMEM((blocks, keys, dim), low),
            pltpu.VMEM((blocks, keys, dim), low),
            pltpu.VMEM((blocks, dim, keys), low),
            pltpu.VMEM((blocks, 1, 640), full),
            pltpu.VMEM((all_keys, dim), full),
            pltpu.VMEM((all_keys, dim), full),
            pltpu.VMEM((all_keys, dim), jnp.int32),
            pltpu.VMEM((1, queries), jnp.int32),
            pltpu.VMEM((all_keys, queries), full),
            pltpu.VMEM((all_keys, queries), full),
            pltpu.VMEM((3, 8, queries), full),
            pltpu.VMEM((8, queries), full),
            pltpu.VMEM((8, queries), full),
            pltpu.VMEM((queries, dim), low),
            pltpu.VMEM((4, 2 * rows, dim), low),
            pltpu.VMEM((all_keys, dim), full),
            pltpu.VMEM((all_keys, dim), full),
            pltpu.VMEM((all_keys, dim), full),
            pltpu.VMEM((6, keys, dim), low),
            pltpu.VMEM((6, keys, dim), low),
            pltpu.VMEM((8, dim), full),
            pltpu.VMEM((7, 8, dim), full),
            dma((5,)),
            dma((7,)),
            dma((3,)),
            dma((3,)),
            dma((3, 2)),
            dma((3, 2)),
            dma((3, 2)),
            dma((3, 2)),
            dma(()),
            dma((4,)),
            dma(()),
            dma((4,)),
            dma((chunks,)),
            dma((chunks,)),
            dma(()),
            dma((4,)),
            dma((6,)),
            dma((6,)),
            dma((7,)),
            dma((7,)),
        ],
        compiler_params=pltpu.CompilerParams(
            collective_id=0, has_side_effects=True, vmem_limit_bytes=60 * 1024 * 1024
        ),
        cost_estimate=pl.CostEstimate(
            flops=10 * all_keys * queries * dim,
            bytes_accessed=8 * queries * dim,
            transcendentals=2 * all_keys * queries,
        ),
    )(
        queries_in,
        grad_output,
        key_states,
        value_states,
        bias_table,
        gap_bucket,
        order,
    )
    return pl.pallas_call(
        place_kernel,
        out_shape=outs,
        in_specs=[vmem] * 4,
        out_specs=(vmem,) * 4,
    )(*results)


def solution(mesh):
    placed = (
        P("row", None),
        P(("col", "depth"), "row"),
        P(("col", "depth"), "row"),
        P("row", None),
        P(),
        P(("col", "depth")),
        P(),
    )
    return jax.shard_map(
        per_device,
        mesh=mesh,
        in_specs=placed,
        out_specs=(
            P("row", ("col", "depth")),
            P(("col", "depth"), "row"),
            P(("col", "depth"), "row"),
            P("row", None),
        ),
        check_vma=False,
    )
```

```python
import functools
import math

import jax
import jax.numpy as jnp
from jax import lax
from jax.experimental import pallas as pl
from jax.experimental.pallas import tpu as pltpu
from jax.sharding import PartitionSpec as P

rows = 144
dim = 128
keys = 576
half_keys = keys // 2
blocks = 4
all_keys = blocks * keys
levels = 64
slots = 8
queries = slots * rows
cuts = (0, 512, 1152)
chunks = len(cuts) - 1
z_steps = (0, 1, 3, 2)
scale = dim ** -0.5
log2e = math.log2(math.e)
masked_value = -1e30
floor_value = -1e20
MESH = pl.DeviceIdType.MESH


def fold(a, combine):
    return combine(a.reshape(a.shape[0] // 8, 8, a.shape[1]), axis=0)


def wide(a, count):
    return jnp.concatenate([a] * (count // dim), axis=1)


def nt_dot(a, b):
    return lax.dot_general(a, b, (((1,), (1,)), ((), ())), preferred_element_type=jnp.float32)


def nn_dot(a, b):
    return jnp.dot(a, b, preferred_element_type=jnp.float32)


def column_of(row):
    pieces = []
    eye = lax.broadcasted_iota(jnp.int32, (dim, dim), 0) == lax.broadcasted_iota(
        jnp.int32, (dim, dim), 1
    )
    for start in range(0, keys, dim):
        spread = jnp.broadcast_to(row[:, start : start + dim], (dim, dim))
        column = jnp.sum(jnp.where(eye, spread, 0.0), axis=1, keepdims=True)
        pieces.append(column[: min(dim, keys - start)])
    return jnp.concatenate(pieces, axis=0)


def merge(parts):
    best = functools.reduce(jnp.maximum, [a[0:1] for a in parts])
    factors = [jnp.exp2(a[0:1] - best) for a in parts]
    total = sum(a[1:2] * f for a, f in zip(parts, factors))
    moment = sum(a[2:3] * f for a, f in zip(parts, factors))
    return best, total, moment


def kernel(
    q_ref,
    g_ref,
    k_ref,
    v_ref,
    table_hbm,
    gap_hbm,
    order_hbm,
    dq_hbm,
    dk_hbm,
    dv_hbm,
    db_hbm,
    dq_out,
    dk_out,
    dv_out,
    db_out,
    table_ref,
    gap_ref,
    order_ref,
    q_all,
    g_all,
    k_all,
    v_all,
    k_turned,
    gap_rows,
    gap_cols,
    bias_cols,
    key_pos,
    query_pos,
    s_all,
    dp_all,
    state,
    stats,
    stats_got,
    dq_all,
    dq_got,
    held,
    dk_sum,
    dv_sum,
    ds_sum,
    kv_low,
    kv_got,
    db_own,
    db_got,
    local_sem,
    store_sem,
    gap_send,
    gap_recv,
    k_send,
    k_recv,
    v_send,
    v_recv,
    q_send,
    q_recv,
    g_send,
    g_recv,
    st_send,
    st_recv,
    dq_send,
    dq_recv,
    held_recv,
    on_send,
    dkv_send,
    dkv_recv,
    db_send,
    db_recv,
):
    row = lax.axis_index("row")
    col = lax.axis_index("col")
    depth = lax.axis_index("depth")
    z_lo = row // 8
    x = (row // 2) % 4
    core = row % 2
    z = depth * 4 + z_lo
    member = col // 2
    parity = col % 2
    other = (core + member) % 2
    own_row = col == 0
    dq_self = (member == 0) & (col == z_lo)

    def shift(j):
        return (parity + (1 if j in (1, 2) else 0)) % 2

    def at(step, xx):
        there = (z + step + 8) % 8
        return ((there % 4) * 8 + xx * 2 + other, col, there // 4)

    def slot_x(s):
        return (x + shift(s // 2) + 2 * (s % 2)) % 4

    def beside(d):
        return (z_lo * 8 + ((x + d) % 4) * 2 + core, col, depth)

    def peer(a, b):
        return (row, (col + a) % 4, (depth + b) % 2)

    loads = [
        pltpu.make_async_copy(src, dst, local_sem.at[n])
        for n, (src, dst) in enumerate(
            (
                (k_ref, k_all.at[0]),
                (v_ref, v_all.at[0]),
                (gap_hbm, gap_ref),
                (table_hbm, table_ref),
                (order_hbm, order_ref),
            )
        )
    ]
    for copy in loads:
        copy.start()

    barrier = pltpu.get_barrier_semaphore()

    def greet(device):
        pl.semaphore_signal(barrier, inc=1, device_id=device, device_id_type=MESH)

    for n in range(8):
        from_col, from_depth = n // 2, n % 2
        head_core = (core + from_col // 2) % 2

        @pl.when(jnp.logical_not(dq_self & (from_col == col) & (depth == from_depth)))
        def _(device=(col * 8 + x * 2 + head_core, from_col, from_depth)):
            greet(device)

    for n in (5, 7, 3, 4, 1, 6, 2):
        greet(peer(n // 2, n % 2))
    for d in (2, 1, 3):
        greet(beside(d))
    for step, j in ((2, 3), (-2, 3), (1, 1), (-1, 2), (0, 0)):
        for i in range(2):
            device = at(step, (x + shift(j) + 2 * i) % 4)
            if step == 0 and i == 0:

                @pl.when(jnp.logical_not(own_row))
                def _(device=device):
                    greet(device)

            else:
                greet(device)
    loads[2].wait()
    gap_rows[0] = jnp.zeros((1, 640), jnp.float32)
    gap_rows[0, 0:1, 0:keys] = gap_ref[...].astype(jnp.float32).reshape(1, keys)

    pl.semaphore_wait(
        barrier,
        28 - own_row.astype(jnp.int32) - dq_self.astype(jnp.int32),
    )

    def remote(src, dst, send_sem, recv_sem, device):
        return pltpu.make_async_remote_copy(
            src_ref=src,
            dst_ref=dst,
            send_sem=send_sem,
            recv_sem=recv_sem,
            device_id=device,
            device_id_type=MESH,
        )

    def gap_copy(a):
        return remote(
            gap_rows.at[0], gap_rows.at[4 - a], gap_send.at[a - 1], gap_recv.at[3 - a], peer(a, 0)
        )

    def own_copy(a, h, src, dst, send, recv):
        part = pl.ds(h * half_keys, half_keys)
        return remote(
            src.at[part, :],
            dst.at[4 - a, part, :],
            send.at[a - 1, h],
            recv.at[3 - a, h],
            peer(a, 0),
        )

    def pass_copy(a, h, dst, send, recv):
        part = pl.ds(h * half_keys, half_keys)
        return remote(
            dst.at[4 - a, part, :], dst.at[2, part, :], send.at[1, h], recv.at[1, h], peer(a, 0)
        )

    gaps = [gap_copy(a) for a in (1, 3, 2)]
    passed, direct, onward = [], [], []
    for h in range(2):
        passed.append(own_copy(1, h, k_ref, k_all, k_send, k_recv))
        passed.append(own_copy(3, h, v_ref, v_all, v_send, v_recv))
        direct.append(own_copy(3, h, k_ref, k_all, k_send, k_recv))
        direct.append(own_copy(1, h, v_ref, v_all, v_send, v_recv))
        onward.append(pass_copy(1, h, k_all, k_send, k_recv))
        onward.append(pass_copy(3, h, v_all, v_send, v_recv))
    for copy in passed:
        copy.start()

    def send_rows(src, dst, send_sem, recv_sem, step, j):
        for i in range(2):
            target = at(step, (x + 3 * shift(j) + 2 * i) % 4)
            src_part = src.at[:, pl.ds(pl.multiple_of(target[0] * dim, dim), dim)]
            dst_part = dst.at[pl.ds((j * 2 + i) * rows, rows), :]
            away = remote(src_part, dst_part, send_sem, recv_sem.at[j], target)
            if step == 0 and i == 0:

                @pl.when(own_row)
                def _(src_part=src_part, dst_part=dst_part):
                    pltpu.make_async_copy(src_part, dst_part, recv_sem.at[j]).start()

                @pl.when(jnp.logical_not(own_row))
                def _(away=away):
                    away.start()

            else:
                away.start()

    send_rows(q_ref, q_all, q_send, q_recv, 0, 0)
    send_rows(g_ref, g_all, g_send, g_recv, 0, 0)
    for copy in gaps:
        copy.start()
    send_rows(q_ref, q_all, q_send, q_recv, -1, 1)
    send_rows(q_ref, q_all, q_send, q_recv, 1, 2)
    send_rows(q_ref, q_all, q_send, q_recv, -2, 3)
    send_rows(g_ref, g_all, g_send, g_recv, -1, 1)
    send_rows(g_ref, g_all, g_send, g_recv, 1, 2)
    send_rows(g_ref, g_all, g_send, g_recv, 2, 3)
    for copy in direct:
        copy.start()

    for n in (0, 1, 3, 4):
        loads[n].wait()

    lane = lax.broadcasted_iota(jnp.int32, (1, queries), 1)
    half = rows // 2
    pos = jnp.zeros((1, queries), jnp.int32)
    for s in range(slots):
        r = ((z_lo + z_steps[s // 2]) % 4) * 8 + slot_x(s) * 2 + other
        for b in range(2):
            low = s * rows + b * half
            inside = (lane >= low) & (lane < low + half)
            pos = jnp.where(inside, order_ref[2 * r + b] * half + lane - low, pos)
    query_pos[...] = pos
    within = lax.broadcasted_iota(jnp.int32, (keys, dim), 0)
    for b in range(blocks):
        key_pos[b * keys : (b + 1) * keys, :] = within + (((col + b) % 4) * 2 + depth) * keys
    level = lax.broadcasted_iota(jnp.int32, (1, levels), 1).astype(jnp.float32)
    table = table_ref[pl.ds(row, 1), :]

    def fill_bias(b):
        start = b * keys
        column = column_of(gap_rows[b, 0:1, :])
        gap_cols[start : start + keys, :] = jnp.broadcast_to(column, (keys, dim))
        bias = jnp.sum(jnp.where(column == level, table, 0.0), axis=1, keepdims=True)
        bias_cols[start : start + keys, :] = jnp.broadcast_to(bias * log2e, (keys, dim))

    def turn(b):
        k_turned[b] = k_all[b].astype(jnp.float32).T.astype(jnp.bfloat16)

    fill_bias(0)
    fresh = jnp.zeros((8, queries), jnp.float32)
    state[0] = fresh + floor_value
    state[1] = fresh
    state[2] = fresh
    turn(0)

    for come, go in zip(passed, onward):
        come.wait_recv()
        go.start()

    def wait_group(buffer, sem, j):
        part = buffer.at[pl.ds(j * 2 * rows, 2 * rows), :]
        pltpu.make_async_copy(part, part, sem.at[j]).wait()

    def first_pass(c, b):
        lo, hi = cuts[c], cuts[c + 1]
        count = hi - lo
        part = slice(b * keys, (b + 1) * keys)
        s = nt_dot(k_all[b], q_all[lo:hi, :]) * (scale * log2e)
        s = s + wide(bias_cols[part, :], count)
        s = jnp.where(wide(key_pos[part, :], count) <= query_pos[:, lo:hi], s, masked_value)
        s_all[part, lo:hi] = s
        dp = nt_dot(v_all[b], g_all[lo:hi, :])
        dp_all[part, lo:hi] = dp
        before = state[0, :, lo:hi]
        best = jnp.maximum(before, fold(s, jnp.max))
        factor = jnp.exp2(before - best)
        w = jnp.exp2(s.reshape(keys // 8, 8, count) - best[None])
        wd = w * dp.reshape(keys // 8, 8, count)
        state[0, :, lo:hi] = best
        state[1, :, lo:hi] = state[1, :, lo:hi] * factor + jnp.sum(w, axis=0)
        state[2, :, lo:hi] = state[2, :, lo:hi] * factor + jnp.sum(wd, axis=0)

    def stat_copy(c):
        part = pl.ds(cuts[c], cuts[c + 1] - cuts[c])
        return remote(
            stats.at[:, part], stats_got.at[:, part], st_send.at[c], st_recv.at[c], peer(0, 1)
        )

    def close(c):
        lo, hi = cuts[c], cuts[c + 1]
        best = jnp.max(state[0, :, lo:hi], axis=0, keepdims=True)
        factor = jnp.exp2(state[0, :, lo:hi] - best)
        stats[0:1, lo:hi] = best
        stats[1:2, lo:hi] = jnp.sum(state[1, :, lo:hi] * factor, axis=0, keepdims=True)
        stats[2:3, lo:hi] = jnp.sum(state[2, :, lo:hi] * factor, axis=0, keepdims=True)
        stat_copy(c).start()

    wait_group(q_all, q_recv, 0)
    wait_group(g_all, g_recv, 0)
    wait_group(q_all, q_recv, 1)
    wait_group(g_all, g_recv, 1)
    first_pass(0, 0)
    for copy in gaps:
        copy.wait_recv()
    for b in (3, 1, 2):
        fill_bias(b)
    for copy in direct:
        copy.wait_recv()
    turn(1)
    turn(3)
    first_pass(0, 1)
    first_pass(0, 3)
    for j in (2, 3):
        wait_group(q_all, q_recv, j)
        wait_group(g_all, g_recv, j)
    for b in (0, 1, 3):
        first_pass(1, b)
    for copy in onward:
        copy.wait_recv()
    for c in range(chunks):
        first_pass(c, 2)
        close(c)
    turn(2)

    def kv_copy(n, a):
        return remote(
            kv_low.at[n], kv_got.at[n], dkv_send.at[n], dkv_recv.at[n], peer(a, 0)
        )

    returns = [kv_copy(n, a) for n, a in enumerate((1, 3, 3, 1, 1, 3))]

    def low(total, b, factor):
        return (total[b * keys : (b + 1) * keys, :] * factor).astype(jnp.bfloat16)

    def slot_d(s):
        return (shift(s // 2) + 2 * (s % 2)) % 4

    def onto(s, src):
        head_x = (x + 4 - slot_d(s)) % 4
        place = (head_x % 2) * 2 + core
        dst = dq_got.at[place, pl.ds(pl.multiple_of(depth * rows, rows), rows), :]
        target = (((z_lo + z_steps[s // 2]) % 4) * 8 + x * 2 + other, z_lo, head_x // 2)
        mine = dq_self & (head_x // 2 == depth) if s // 2 == 0 else None
        return remote(src, dst, on_send.at[s], dq_recv.at[place], target), mine, place, dst

    def send_on(s, src):
        away, mine, place, dst = onto(s, src)
        if mine is None:
            away.start()
        else:

            @pl.when(mine)
            def _():
                pltpu.make_async_copy(src, dst, dq_recv.at[place]).start()

            @pl.when(jnp.logical_not(mine))
            def _():
                away.start()

    def hand_on(s):
        def go():
            pltpu.make_async_copy(held.at[s], held.at[s], held_recv.at[s]).wait()
            send_on(s, held.at[s])

        if s % 2:
            go()
        else:
            pl.when(shift(s // 2) == 1)(go)

    def factors(c):
        lo, hi = cuts[c], cuts[c + 1]
        stat_copy(c).wait()
        best, total, moment = merge([stats[0:3, lo:hi], stats_got[0:3, lo:hi]])
        return best + jnp.log(total) * log2e, moment / total

    def grads(c, b, lse, delta):
        lo, hi = cuts[c], cuts[c + 1]
        part = slice(b * keys, (b + 1) * keys)
        p = jnp.exp2(s_all[part, lo:hi] - lse)
        ds = p * (dp_all[part, lo:hi] - delta)
        ds_lanes = sum(ds[:, n * dim : (n + 1) * dim] for n in range((hi - lo) // dim))
        ds_low = ds.astype(jnp.bfloat16)
        dv_part = nn_dot(p.astype(jnp.bfloat16), g_all[lo:hi, :])
        dk_part = nn_dot(ds_low, q_all[lo:hi, :])
        if c == 0:
            ds_sum[part, :] = ds_lanes
            dv_sum[part, :] = dv_part
            dk_sum[part, :] = dk_part
        else:
            ds_sum[part, :] += ds_lanes
            dv_sum[part, :] += dv_part
            dk_sum[part, :] += dk_part
        return nn_dot(k_turned[b], ds_low)

    def send_dq(c, dq):
        dq_all[cuts[c] : cuts[c + 1], :] = (dq.T * scale).astype(jnp.bfloat16)
        for s in range(cuts[c] // rows, cuts[c + 1] // rows):
            src = dq_all.at[pl.ds(s * rows, rows), :]
            aside = remote(src, held.at[s], dq_send, held_recv.at[s], beside(slot_d(s)))
            if s % 2:
                aside.start()
            else:

                @pl.when(shift(s // 2) == 0)
                def _(s=s, src=src):
                    send_on(s, src)

                @pl.when(shift(s // 2) == 1)
                def _(aside=aside):
                    aside.start()

    def send_kv(n, total, b, factor):
        kv_low[n] = low(total, b, factor)
        returns[n].start()

    lse, delta = factors(0)
    send_dq(0, sum(grads(0, b, lse, delta) for b in (2, 3, 1, 0)))
    lse, delta = factors(1)
    dq = grads(1, 2, lse, delta)
    send_kv(0, dk_sum, 2, scale)
    send_kv(1, dv_sum, 2, 1.0)
    dq = dq + grads(1, 3, lse, delta)
    send_kv(2, dk_sum, 3, scale)
    dq = dq + grads(1, 1, lse, delta)
    send_kv(3, dv_sum, 1, 1.0)
    send_dq(1, dq + grads(1, 0, lse, delta))

    column = jnp.sum(ds_sum[...], axis=1, keepdims=True)
    by_level = jnp.where(gap_cols[:, 0:levels] == level, column, 0.0)
    db_own[...] = jnp.zeros_like(db_own)
    db_own[0:1, 0:levels] = jnp.sum(by_level, axis=0, keepdims=True)
    biases = [
        remote(db_own, db_got.at[n - 1], db_send.at[n - 1], db_recv.at[n - 1], peer(n // 2, n % 2))
        for n in range(1, 8)
    ]
    for copy in biases:
        copy.start()

    for s in range(3):
        hand_on(s)
    returns[0].wait_recv()
    kv_low[4] = (dk_sum[keys : 2 * keys, :] * scale + kv_got[0].astype(jnp.float32)).astype(
        jnp.bfloat16
    )
    returns[4].start()
    returns[1].wait_recv()
    kv_low[5] = (dv_sum[3 * keys : 4 * keys, :] + kv_got[1].astype(jnp.float32)).astype(
        jnp.bfloat16
    )
    returns[5].start()
    for s in range(3, slots):
        hand_on(s)

    stores = [
        pltpu.make_async_copy(src, dst, store_sem.at[n])
        for n, (src, dst) in enumerate(((dk_out, dk_hbm), (dv_out, dv_hbm), (db_out, db_hbm)))
    ]
    returns[2].wait_recv()
    returns[4].wait_recv()
    dk_out[...] = (
        dk_sum[0:keys, :] * scale + kv_got[2].astype(jnp.float32) + kv_got[4].astype(jnp.float32)
    )
    stores[0].start()
    returns[3].wait_recv()
    returns[5].wait_recv()
    dv_out[...] = (
        dv_sum[0:keys, :] + kv_got[3].astype(jnp.float32) + kv_got[5].astype(jnp.float32)
    )
    stores[1].start()
    for copy in biases:
        copy.wait()
    db_out[...] = db_own[0:1, 0:levels] + sum(db_got[n, 0:1, 0:levels] for n in range(7))
    stores[2].start()

    for head in range(4):
        both = dq_got.at[head]
        pltpu.make_async_copy(both, both, dq_recv.at[head]).wait()
        dq_out[:, head * dim : (head + 1) * dim] = both[0:rows, :].astype(jnp.float32) + both[
            rows : 2 * rows, :
        ].astype(jnp.float32)
        part = pl.ds(head * dim, dim)
        stores.append(
            pltpu.make_async_copy(dq_out.at[:, part], dq_hbm.at[:, part], store_sem.at[3 + head])
        )
        stores[3 + head].start()

    def drain(buffer, sem, short):
        @pl.when(short)
        def _():
            part = buffer.at[pl.ds(0, queries - rows), :]
            pltpu.make_async_copy(part, part, sem).wait()

        @pl.when(jnp.logical_not(short))
        def _():
            pltpu.make_async_copy(buffer, buffer, sem).wait()

    drain(q_all, q_send, own_row)
    drain(g_all, g_send, own_row)
    part = dq_all.at[pl.ds(0, 6 * rows), :]
    pltpu.make_async_copy(part, part, dq_send).wait()
    for s in range(slots):
        away, mine, _, _ = onto(s, held.at[s])
        if mine is None:
            away.wait_send()
        else:
            pl.when(jnp.logical_not(mine))(away.wait_send)

    for copy in stores:
        copy.wait()
    for copy in gaps + passed + direct + onward + returns:
        copy.wait_send()


def place_kernel(dq, dk, dv, db, dq_out, dk_out, dv_out, db_out):
    dq_out[...] = dq[...]
    dk_out[...] = dk[...]
    dv_out[...] = dv[...]
    db_out[...] = db[...]


def per_device(queries_in, key_states, value_states, grad_output, bias_table, gap_bucket, order):
    vmem = pl.BlockSpec(memory_space=pltpu.VMEM)
    hbm = pl.BlockSpec(memory_space=pltpu.HBM)
    low, full = jnp.bfloat16, jnp.float32
    dma = pltpu.SemaphoreType.DMA
    outs = (
        jax.ShapeDtypeStruct((rows, 4 * dim), full),
        jax.ShapeDtypeStruct((keys, dim), full),
        jax.ShapeDtypeStruct((keys, dim), full),
        jax.ShapeDtypeStruct((1, levels), full),
    )
    results = pl.pallas_call(
        kernel,
        out_shape=outs,
        in_specs=[
            hbm,
            hbm,
            hbm,
            hbm,
            hbm,
            hbm,
            hbm,
        ],
        out_specs=(hbm, hbm, hbm, hbm),
        scratch_shapes=[pltpu.VMEM(a.shape, full) for a in outs]
        + [
            pltpu.VMEM((32, levels), full),
            pltpu.VMEM((keys,), jnp.int32),
            pltpu.SMEM((64,), jnp.int32),
            pltpu.VMEM((queries, dim), low),
            pltpu.VMEM((queries, dim), low),
            pltpu.VMEM((blocks, keys, dim), low),
            pltpu.VMEM((blocks, keys, dim), low),
            pltpu.VMEM((blocks, dim, keys), low),
            pltpu.VMEM((blocks, 1, 640), full),
            pltpu.VMEM((all_keys, dim), full),
            pltpu.VMEM((all_keys, dim), full),
            pltpu.VMEM((all_keys, dim), jnp.int32),
            pltpu.VMEM((1, queries), jnp.int32),
            pltpu.VMEM((all_keys, queries), full),
            pltpu.VMEM((all_keys, queries), full),
            pltpu.VMEM((3, 8, queries), full),
            pltpu.VMEM((8, queries), full),
            pltpu.VMEM((8, queries), full),
            pltpu.VMEM((queries, dim), low),
            pltpu.VMEM((4, 2 * rows, dim), low),
            pltpu.VMEM((slots, rows, dim), low),
            pltpu.VMEM((all_keys, dim), full),
            pltpu.VMEM((all_keys, dim), full),
            pltpu.VMEM((all_keys, dim), full),
            pltpu.VMEM((6, keys, dim), low),
            pltpu.VMEM((6, keys, dim), low),
            pltpu.VMEM((8, dim), full),
            pltpu.VMEM((7, 8, dim), full),
            dma((5,)),
            dma((7,)),
            dma((3,)),
            dma((3,)),
            dma((3, 2)),
            dma((3, 2)),
            dma((3, 2)),
            dma((3, 2)),
            dma(()),
            dma((4,)),
            dma(()),
            dma((4,)),
            dma((chunks,)),
            dma((chunks,)),
            dma(()),
            dma((4,)),
            dma((slots,)),
            dma((slots,)),
            dma((6,)),
            dma((6,)),
            dma((7,)),
            dma((7,)),
        ],
        compiler_params=pltpu.CompilerParams(
            collective_id=0, has_side_effects=True, vmem_limit_bytes=60 * 1024 * 1024
        ),
        cost_estimate=pl.CostEstimate(
            flops=10 * all_keys * queries * dim,
            bytes_accessed=8 * queries * dim,
            transcendentals=2 * all_keys * queries,
        ),
    )(
        queries_in,
        grad_output,
        key_states,
        value_states,
        bias_table,
        gap_bucket,
        order,
    )
    return pl.pallas_call(
        place_kernel,
        out_shape=outs,
        in_specs=[vmem] * 4,
        out_specs=(vmem,) * 4,
    )(*results)


def solution(mesh):
    placed = (
        P("row", None),
        P(("col", "depth"), "row"),
        P(("col", "depth"), "row"),
        P("row", None),
        P(),
        P(("col", "depth")),
        P(),
    )
    return jax.shard_map(
        per_device,
        mesh=mesh,
        in_specs=placed,
        out_specs=(
            P("row", ("col", "depth")),
            P(("col", "depth"), "row"),
            P(("col", "depth"), "row"),
            P("row", None),
        ),
        check_vma=False,
    )
```

```python
import functools
import math

import jax
import jax.numpy as jnp
from jax import lax
from jax.experimental import pallas as pl
from jax.experimental.pallas import tpu as pltpu
from jax.sharding import PartitionSpec as P

rows = 144
dim = 128
keys = 576
half_keys = keys // 2
blocks = 4
all_keys = blocks * keys
levels = 64
slots = 8
queries = slots * rows
cuts = (0, 512, 1152)
chunks = len(cuts) - 1
z_steps = (0, 1, 3, 2)
scale = dim ** -0.5
log2e = math.log2(math.e)
masked_value = -1e30
floor_value = -1e20
MESH = pl.DeviceIdType.MESH


def fold(a, combine):
    return combine(a.reshape(a.shape[0] // 8, 8, a.shape[1]), axis=0)


def wide(a, count):
    return jnp.concatenate([a] * (count // dim), axis=1)


def nt_dot(a, b):
    return lax.dot_general(a, b, (((1,), (1,)), ((), ())), preferred_element_type=jnp.float32)


def nn_dot(a, b):
    return jnp.dot(a, b, preferred_element_type=jnp.float32)


def column_of(row):
    pieces = []
    eye = lax.broadcasted_iota(jnp.int32, (dim, dim), 0) == lax.broadcasted_iota(
        jnp.int32, (dim, dim), 1
    )
    for start in range(0, keys, dim):
        spread = jnp.broadcast_to(row[:, start : start + dim], (dim, dim))
        column = jnp.sum(jnp.where(eye, spread, 0.0), axis=1, keepdims=True)
        pieces.append(column[: min(dim, keys - start)])
    return jnp.concatenate(pieces, axis=0)


def merge(parts):
    best = functools.reduce(jnp.maximum, [a[0:1] for a in parts])
    factors = [jnp.exp2(a[0:1] - best) for a in parts]
    total = sum(a[1:2] * f for a, f in zip(parts, factors))
    moment = sum(a[2:3] * f for a, f in zip(parts, factors))
    return best, total, moment


def kernel(
    q_ref,
    g_ref,
    k_ref,
    v_ref,
    table_hbm,
    gap_hbm,
    order_hbm,
    dq_got,
    dk_hbm,
    dv_hbm,
    db_hbm,
    dk_out,
    dv_out,
    db_out,
    table_ref,
    gap_ref,
    order_ref,
    q_all,
    g_all,
    k_all,
    v_all,
    k_turned,
    gap_rows,
    gap_cols,
    bias_cols,
    key_pos,
    query_pos,
    s_all,
    dp_all,
    state,
    stats,
    stats_got,
    dq_all,
    held,
    dk_sum,
    dv_sum,
    ds_sum,
    kv_low,
    kv_got,
    db_own,
    db_got,
    local_sem,
    store_sem,
    gap_send,
    gap_recv,
    k_send,
    k_recv,
    v_send,
    v_recv,
    q_send,
    q_recv,
    g_send,
    g_recv,
    st_send,
    st_recv,
    dq_send,
    dq_recv,
    held_recv,
    on_send,
    dkv_send,
    dkv_recv,
    db_send,
    db_recv,
):
    row = lax.axis_index("row")
    col = lax.axis_index("col")
    depth = lax.axis_index("depth")
    z_lo = row // 8
    x = (row // 2) % 4
    core = row % 2
    z = depth * 4 + z_lo
    member = col // 2
    parity = col % 2
    other = (core + member) % 2
    own_row = col == 0
    dq_self = (member == 0) & (col == z_lo)

    def shift(j):
        return (parity + (1 if j in (1, 2) else 0)) % 2

    def at(step, xx):
        there = (z + step + 8) % 8
        return ((there % 4) * 8 + xx * 2 + other, col, there // 4)

    def slot_x(s):
        return (x + shift(s // 2) + 2 * (s % 2)) % 4

    def beside(d):
        return (z_lo * 8 + ((x + d) % 4) * 2 + core, col, depth)

    def peer(a, b):
        return (row, (col + a) % 4, (depth + b) % 2)

    loads = [
        pltpu.make_async_copy(src, dst, local_sem.at[n])
        for n, (src, dst) in enumerate(
            (
                (k_ref, k_all.at[0]),
                (v_ref, v_all.at[0]),
                (gap_hbm, gap_ref),
                (table_hbm, table_ref),
                (order_hbm, order_ref),
            )
        )
    ]
    for copy in loads:
        copy.start()

    barrier = pltpu.get_barrier_semaphore()

    def greet(device):
        pl.semaphore_signal(barrier, inc=1, device_id=device, device_id_type=MESH)

    for n in range(8):
        from_col, from_depth = n // 2, n % 2
        head_core = (core + from_col // 2) % 2

        @pl.when(jnp.logical_not(dq_self & (from_col == col) & (depth == from_depth)))
        def _(device=(col * 8 + x * 2 + head_core, from_col, from_depth)):
            greet(device)

    for n in (5, 7, 3, 4, 1, 6, 2):
        greet(peer(n // 2, n % 2))
    for d in (2, 1, 3):
        greet(beside(d))
    for step, j in ((2, 3), (-2, 3), (1, 1), (-1, 2), (0, 0)):
        for i in range(2):
            device = at(step, (x + shift(j) + 2 * i) % 4)
            if step == 0 and i == 0:

                @pl.when(jnp.logical_not(own_row))
                def _(device=device):
                    greet(device)

            else:
                greet(device)
    loads[2].wait()
    gap_rows[0] = jnp.zeros((1, 640), jnp.float32)
    gap_rows[0, 0:1, 0:keys] = gap_ref[...].astype(jnp.float32).reshape(1, keys)

    pl.semaphore_wait(
        barrier,
        28 - own_row.astype(jnp.int32) - dq_self.astype(jnp.int32),
    )

    def remote(src, dst, send_sem, recv_sem, device):
        return pltpu.make_async_remote_copy(
            src_ref=src,
            dst_ref=dst,
            send_sem=send_sem,
            recv_sem=recv_sem,
            device_id=device,
            device_id_type=MESH,
        )

    def gap_copy(a):
        return remote(
            gap_rows.at[0], gap_rows.at[4 - a], gap_send.at[a - 1], gap_recv.at[3 - a], peer(a, 0)
        )

    def own_copy(a, h, src, dst, send, recv):
        part = pl.ds(h * half_keys, half_keys)
        return remote(
            src.at[part, :],
            dst.at[4 - a, part, :],
            send.at[a - 1, h],
            recv.at[3 - a, h],
            peer(a, 0),
        )

    def pass_copy(a, h, dst, send, recv):
        part = pl.ds(h * half_keys, half_keys)
        return remote(
            dst.at[4 - a, part, :], dst.at[2, part, :], send.at[1, h], recv.at[1, h], peer(a, 0)
        )

    gaps = [gap_copy(a) for a in (1, 3, 2)]
    passed, direct, onward = [], [], []
    for h in range(2):
        passed.append(own_copy(1, h, k_ref, k_all, k_send, k_recv))
        passed.append(own_copy(3, h, v_ref, v_all, v_send, v_recv))
        direct.append(own_copy(3, h, k_ref, k_all, k_send, k_recv))
        direct.append(own_copy(1, h, v_ref, v_all, v_send, v_recv))
        onward.append(pass_copy(1, h, k_all, k_send, k_recv))
        onward.append(pass_copy(3, h, v_all, v_send, v_recv))
    for copy in passed:
        copy.start()

    def send_rows(src, dst, send_sem, recv_sem, step, j):
        for i in range(2):
            target = at(step, (x + 3 * shift(j) + 2 * i) % 4)
            src_part = src.at[:, pl.ds(pl.multiple_of(target[0] * dim, dim), dim)]
            dst_part = dst.at[pl.ds((j * 2 + i) * rows, rows), :]
            away = remote(src_part, dst_part, send_sem, recv_sem.at[j], target)
            if step == 0 and i == 0:

                @pl.when(own_row)
                def _(src_part=src_part, dst_part=dst_part):
                    pltpu.make_async_copy(src_part, dst_part, recv_sem.at[j]).start()

                @pl.when(jnp.logical_not(own_row))
                def _(away=away):
                    away.start()

            else:
                away.start()

    send_rows(q_ref, q_all, q_send, q_recv, 0, 0)
    send_rows(g_ref, g_all, g_send, g_recv, 0, 0)
    for copy in gaps:
        copy.start()
    send_rows(q_ref, q_all, q_send, q_recv, -1, 1)
    send_rows(g_ref, g_all, g_send, g_recv, -1, 1)
    send_rows(q_ref, q_all, q_send, q_recv, 1, 2)
    send_rows(g_ref, g_all, g_send, g_recv, 1, 2)
    send_rows(q_ref, q_all, q_send, q_recv, -2, 3)
    send_rows(g_ref, g_all, g_send, g_recv, 2, 3)
    for copy in direct:
        copy.start()

    for n in (0, 1, 3, 4):
        loads[n].wait()

    lane = lax.broadcasted_iota(jnp.int32, (1, queries), 1)
    half = rows // 2
    pos = jnp.zeros((1, queries), jnp.int32)
    for s in range(slots):
        r = ((z_lo + z_steps[s // 2]) % 4) * 8 + slot_x(s) * 2 + other
        for b in range(2):
            low = s * rows + b * half
            inside = (lane >= low) & (lane < low + half)
            pos = jnp.where(inside, order_ref[2 * r + b] * half + lane - low, pos)
    query_pos[...] = pos
    within = lax.broadcasted_iota(jnp.int32, (keys, dim), 0)
    for b in range(blocks):
        key_pos[b * keys : (b + 1) * keys, :] = within + (((col + b) % 4) * 2 + depth) * keys
    level = lax.broadcasted_iota(jnp.int32, (1, levels), 1).astype(jnp.float32)
    table = table_ref[pl.ds(row, 1), :]

    def fill_bias(b):
        start = b * keys
        column = column_of(gap_rows[b, 0:1, :])
        gap_cols[start : start + keys, :] = jnp.broadcast_to(column, (keys, dim))
        bias = jnp.sum(jnp.where(column == level, table, 0.0), axis=1, keepdims=True)
        bias_cols[start : start + keys, :] = jnp.broadcast_to(bias * log2e, (keys, dim))

    def turn(b):
        k_turned[b] = k_all[b].astype(jnp.float32).T.astype(jnp.bfloat16)

    fill_bias(0)
    fresh = jnp.zeros((8, queries), jnp.float32)
    state[0] = fresh + floor_value
    state[1] = fresh
    state[2] = fresh
    turn(0)

    for come, go in zip(passed, onward):
        come.wait_recv()
        go.start()
    for copy in gaps:
        copy.wait_recv()
    for b in (3, 1, 2):
        fill_bias(b)

    def wait_group(buffer, sem, j):
        part = buffer.at[pl.ds(j * 2 * rows, 2 * rows), :]
        pltpu.make_async_copy(part, part, sem.at[j]).wait()

    def first_pass(c, b):
        lo, hi = cuts[c], cuts[c + 1]
        count = hi - lo
        part = slice(b * keys, (b + 1) * keys)
        s = nt_dot(k_all[b], q_all[lo:hi, :]) * (scale * log2e)
        s = s + wide(bias_cols[part, :], count)
        s = jnp.where(wide(key_pos[part, :], count) <= query_pos[:, lo:hi], s, masked_value)
        s_all[part, lo:hi] = s
        dp = nt_dot(v_all[b], g_all[lo:hi, :])
        dp_all[part, lo:hi] = dp
        before = state[0, :, lo:hi]
        best = jnp.maximum(before, fold(s, jnp.max))
        factor = jnp.exp2(before - best)
        w = jnp.exp2(s.reshape(keys // 8, 8, count) - best[None])
        wd = w * dp.reshape(keys // 8, 8, count)
        state[0, :, lo:hi] = best
        state[1, :, lo:hi] = state[1, :, lo:hi] * factor + jnp.sum(w, axis=0)
        state[2, :, lo:hi] = state[2, :, lo:hi] * factor + jnp.sum(wd, axis=0)

    def stat_copy(c):
        part = pl.ds(cuts[c], cuts[c + 1] - cuts[c])
        return remote(
            stats.at[:, part], stats_got.at[:, part], st_send.at[c], st_recv.at[c], peer(0, 1)
        )

    def close(c):
        lo, hi = cuts[c], cuts[c + 1]
        best = jnp.max(state[0, :, lo:hi], axis=0, keepdims=True)
        factor = jnp.exp2(state[0, :, lo:hi] - best)
        stats[0:1, lo:hi] = best
        stats[1:2, lo:hi] = jnp.sum(state[1, :, lo:hi] * factor, axis=0, keepdims=True)
        stats[2:3, lo:hi] = jnp.sum(state[2, :, lo:hi] * factor, axis=0, keepdims=True)
        stat_copy(c).start()

    wait_group(q_all, q_recv, 0)
    wait_group(g_all, g_recv, 0)
    wait_group(q_all, q_recv, 1)
    wait_group(g_all, g_recv, 1)
    first_pass(0, 0)
    for copy in direct:
        copy.wait_recv()
    first_pass(0, 1)
    first_pass(0, 3)
    for j in (2, 3):
        wait_group(q_all, q_recv, j)
        wait_group(g_all, g_recv, j)
    for b in (0, 1, 3):
        first_pass(1, b)
    for copy in onward:
        copy.wait_recv()
    for c in range(chunks):
        first_pass(c, 2)
        close(c)
    for b in (2, 3, 1):
        turn(b)

    def kv_copy(n, a):
        return remote(
            kv_low.at[n], kv_got.at[n], dkv_send.at[n], dkv_recv.at[n], peer(a, 0)
        )

    returns = [kv_copy(n, a) for n, a in enumerate((1, 3, 3, 1, 1, 3))]

    def low(total, b, factor):
        return (total[b * keys : (b + 1) * keys, :] * factor).astype(jnp.bfloat16)

    def slot_d(s):
        return (shift(s // 2) + 2 * (s % 2)) % 4

    def onto(s, src):
        head_x = (x + 4 - slot_d(s)) % 4
        place = (head_x % 2) * 2 + core
        dst = dq_got.at[place, pl.ds(pl.multiple_of(depth * rows, rows), rows), :]
        target = (((z_lo + z_steps[s // 2]) % 4) * 8 + x * 2 + other, z_lo, head_x // 2)
        mine = dq_self & (head_x // 2 == depth) if s // 2 == 0 else None
        return remote(src, dst, on_send.at[s], dq_recv.at[place], target), mine, place, dst

    def send_on(s, src):
        away, mine, place, dst = onto(s, src)
        if mine is None:
            away.start()
        else:

            @pl.when(mine)
            def _():
                pltpu.make_async_copy(src, dst, dq_recv.at[place]).start()

            @pl.when(jnp.logical_not(mine))
            def _():
                away.start()

    def hand_on(s):
        def go():
            pltpu.make_async_copy(held.at[s], held.at[s], held_recv.at[s]).wait()
            send_on(s, held.at[s])

        if s % 2:
            go()
        else:
            pl.when(shift(s // 2) == 1)(go)

    def factors(c):
        lo, hi = cuts[c], cuts[c + 1]
        stat_copy(c).wait()
        best, total, moment = merge([stats[0:3, lo:hi], stats_got[0:3, lo:hi]])
        return best + jnp.log(total) * log2e, moment / total

    def grads(c, b, lse, delta):
        lo, hi = cuts[c], cuts[c + 1]
        part = slice(b * keys, (b + 1) * keys)
        p = jnp.exp2(s_all[part, lo:hi] - lse)
        ds = p * (dp_all[part, lo:hi] - delta)
        ds_lanes = sum(ds[:, n * dim : (n + 1) * dim] for n in range((hi - lo) // dim))
        ds_low = ds.astype(jnp.bfloat16)
        dv_part = nn_dot(p.astype(jnp.bfloat16), g_all[lo:hi, :])
        dk_part = nn_dot(ds_low, q_all[lo:hi, :])
        if c == 0:
            ds_sum[part, :] = ds_lanes
            dv_sum[part, :] = dv_part
            dk_sum[part, :] = dk_part
        else:
            ds_sum[part, :] += ds_lanes
            dv_sum[part, :] += dv_part
            dk_sum[part, :] += dk_part
        return nn_dot(k_turned[b], ds_low)

    def send_dq(c, dq):
        dq_all[cuts[c] : cuts[c + 1], :] = (dq.T * scale).astype(jnp.bfloat16)
        for s in range(cuts[c] // rows, cuts[c + 1] // rows):
            src = dq_all.at[pl.ds(s * rows, rows), :]
            aside = remote(src, held.at[s], dq_send, held_recv.at[s], beside(slot_d(s)))
            if s % 2:
                aside.start()
            else:

                @pl.when(shift(s // 2) == 0)
                def _(s=s, src=src):
                    send_on(s, src)

                @pl.when(shift(s // 2) == 1)
                def _(aside=aside):
                    aside.start()

    def send_kv(n, total, b, factor):
        kv_low[n] = low(total, b, factor)
        returns[n].start()

    lse, delta = factors(0)
    send_dq(0, sum(grads(0, b, lse, delta) for b in (2, 3, 1, 0)))
    lse, delta = factors(1)
    dq = grads(1, 2, lse, delta)
    send_kv(0, dk_sum, 2, scale)
    send_kv(1, dv_sum, 2, 1.0)
    dq = dq + grads(1, 3, lse, delta)
    send_kv(2, dk_sum, 3, scale)
    dq = dq + grads(1, 1, lse, delta)
    send_kv(3, dv_sum, 1, 1.0)
    send_dq(1, dq + grads(1, 0, lse, delta))

    column = jnp.sum(ds_sum[...], axis=1, keepdims=True)
    by_level = jnp.where(gap_cols[:, 0:levels] == level, column, 0.0)
    db_own[...] = jnp.zeros_like(db_own)
    db_own[0:1, 0:levels] = jnp.sum(by_level, axis=0, keepdims=True)
    biases = [
        remote(db_own, db_got.at[n - 1], db_send.at[n - 1], db_recv.at[n - 1], peer(n // 2, n % 2))
        for n in range(1, 8)
    ]
    for copy in biases:
        copy.start()

    for s in range(3):
        hand_on(s)
    returns[0].wait_recv()
    kv_low[4] = (dk_sum[keys : 2 * keys, :] * scale + kv_got[0].astype(jnp.float32)).astype(
        jnp.bfloat16
    )
    returns[4].start()
    returns[1].wait_recv()
    kv_low[5] = (dv_sum[3 * keys : 4 * keys, :] + kv_got[1].astype(jnp.float32)).astype(
        jnp.bfloat16
    )
    returns[5].start()
    for s in range(3, slots):
        hand_on(s)

    stores = [
        pltpu.make_async_copy(src, dst, store_sem.at[n])
        for n, (src, dst) in enumerate(((dk_out, dk_hbm), (dv_out, dv_hbm), (db_out, db_hbm)))
    ]
    returns[2].wait_recv()
    returns[4].wait_recv()
    dk_out[...] = (
        dk_sum[0:keys, :] * scale + kv_got[2].astype(jnp.float32) + kv_got[4].astype(jnp.float32)
    )
    stores[0].start()
    returns[3].wait_recv()
    returns[5].wait_recv()
    dv_out[...] = (
        dv_sum[0:keys, :] + kv_got[3].astype(jnp.float32) + kv_got[5].astype(jnp.float32)
    )
    stores[1].start()
    for copy in biases:
        copy.wait()
    db_out[...] = db_own[0:1, 0:levels] + sum(db_got[n, 0:1, 0:levels] for n in range(7))
    stores[2].start()

    for head in range(4):
        both = dq_got.at[head]
        pltpu.make_async_copy(both, both, dq_recv.at[head]).wait()

    def drain(buffer, sem, short):
        @pl.when(short)
        def _():
            part = buffer.at[pl.ds(0, queries - rows), :]
            pltpu.make_async_copy(part, part, sem).wait()

        @pl.when(jnp.logical_not(short))
        def _():
            pltpu.make_async_copy(buffer, buffer, sem).wait()

    drain(q_all, q_send, own_row)
    drain(g_all, g_send, own_row)
    part = dq_all.at[pl.ds(0, 6 * rows), :]
    pltpu.make_async_copy(part, part, dq_send).wait()
    for s in range(slots):
        away, mine, _, _ = onto(s, held.at[s])
        if mine is None:
            away.wait_send()
        else:
            pl.when(jnp.logical_not(mine))(away.wait_send)

    for copy in stores:
        copy.wait()
    for copy in gaps + passed + direct + onward + returns:
        copy.wait_send()


def place_kernel(dq, dk, dv, db, dq_out, dk_out, dv_out, db_out):
    for head in range(4):
        dq_out[:, head * dim : (head + 1) * dim] = dq[head, 0:rows, :].astype(
            jnp.float32
        ) + dq[head, rows : 2 * rows, :].astype(jnp.float32)
    dk_out[...] = dk[...]
    dv_out[...] = dv[...]
    db_out[...] = db[...]


def per_device(queries_in, key_states, value_states, grad_output, bias_table, gap_bucket, order):
    vmem = pl.BlockSpec(memory_space=pltpu.VMEM)
    hbm = pl.BlockSpec(memory_space=pltpu.HBM)
    low, full = jnp.bfloat16, jnp.float32
    dma = pltpu.SemaphoreType.DMA
    outs = (
        jax.ShapeDtypeStruct((rows, 4 * dim), full),
        jax.ShapeDtypeStruct((keys, dim), full),
        jax.ShapeDtypeStruct((keys, dim), full),
        jax.ShapeDtypeStruct((1, levels), full),
    )
    results = pl.pallas_call(
        kernel,
        out_shape=(jax.ShapeDtypeStruct((4, 2 * rows, dim), low),) + outs[1:],
        in_specs=[
            hbm,
            hbm,
            hbm,
            hbm,
            hbm,
            hbm,
            hbm,
        ],
        out_specs=(hbm, hbm, hbm, hbm),
        scratch_shapes=[pltpu.VMEM(a.shape, full) for a in outs[1:]]
        + [
            pltpu.VMEM((32, levels), full),
            pltpu.VMEM((keys,), jnp.int32),
            pltpu.SMEM((64,), jnp.int32),
            pltpu.VMEM((queries, dim), low),
            pltpu.VMEM((queries, dim), low),
            pltpu.VMEM((blocks, keys, dim), low),
            pltpu.VMEM((blocks, keys, dim), low),
            pltpu.VMEM((blocks, dim, keys), low),
            pltpu.VMEM((blocks, 1, 640), full),
            pltpu.VMEM((all_keys, dim), full),
            pltpu.VMEM((all_keys, dim), full),
            pltpu.VMEM((all_keys, dim), jnp.int32),
            pltpu.VMEM((1, queries), jnp.int32),
            pltpu.VMEM((all_keys, queries), full),
            pltpu.VMEM((all_keys, queries), full),
            pltpu.VMEM((3, 8, queries), full),
            pltpu.VMEM((8, queries), full),
            pltpu.VMEM((8, queries), full),
            pltpu.VMEM((queries, dim), low),
            pltpu.VMEM((slots, rows, dim), low),
            pltpu.VMEM((all_keys, dim), full),
            pltpu.VMEM((all_keys, dim), full),
            pltpu.VMEM((all_keys, dim), full),
            pltpu.VMEM((6, keys, dim), low),
            pltpu.VMEM((6, keys, dim), low),
            pltpu.VMEM((8, dim), full),
            pltpu.VMEM((7, 8, dim), full),
            dma((5,)),
            dma((3,)),
            dma((3,)),
            dma((3,)),
            dma((3, 2)),
            dma((3, 2)),
            dma((3, 2)),
            dma((3, 2)),
            dma(()),
            dma((4,)),
            dma(()),
            dma((4,)),
            dma((chunks,)),
            dma((chunks,)),
            dma(()),
            dma((4,)),
            dma((slots,)),
            dma((slots,)),
            dma((6,)),
            dma((6,)),
            dma((7,)),
            dma((7,)),
        ],
        compiler_params=pltpu.CompilerParams(
            collective_id=0, has_side_effects=True, vmem_limit_bytes=60 * 1024 * 1024
        ),
        cost_estimate=pl.CostEstimate(
            flops=10 * all_keys * queries * dim,
            bytes_accessed=8 * queries * dim,
            transcendentals=2 * all_keys * queries,
        ),
    )(
        queries_in,
        grad_output,
        key_states,
        value_states,
        bias_table,
        gap_bucket,
        order,
    )
    return pl.pallas_call(
        place_kernel,
        out_shape=outs,
        in_specs=[vmem] * 4,
        out_specs=(vmem,) * 4,
    )(*results)


def solution(mesh):
    placed = (
        P("row", None),
        P(("col", "depth"), "row"),
        P(("col", "depth"), "row"),
        P("row", None),
        P(),
        P(("col", "depth")),
        P(),
    )
    return jax.shard_map(
        per_device,
        mesh=mesh,
        in_specs=placed,
        out_specs=(
            P("row", ("col", "depth")),
            P(("col", "depth"), "row"),
            P(("col", "depth"), "row"),
            P("row", None),
        ),
        check_vma=False,
    )
```

```python
import functools
import math

import jax
import jax.numpy as jnp
from jax import lax
from jax.experimental import pallas as pl
from jax.experimental.pallas import tpu as pltpu
from jax.sharding import PartitionSpec as P

rows = 144
dim = 128
keys = 576
half_keys = keys // 2
blocks = 4
all_keys = blocks * keys
levels = 64
slots = 8
queries = slots * rows
cuts = (0, 512, 1152)
chunks = len(cuts) - 1
z_steps = (0, 1, 3, 2)
scale = dim ** -0.5
log2e = math.log2(math.e)
masked_value = -1e30
floor_value = -1e20
MESH = pl.DeviceIdType.MESH


def fold(a, combine):
    return combine(a.reshape(a.shape[0] // 8, 8, a.shape[1]), axis=0)


def wide(a, count):
    return jnp.concatenate([a] * (count // dim), axis=1)


def nt_dot(a, b):
    return lax.dot_general(a, b, (((1,), (1,)), ((), ())), preferred_element_type=jnp.float32)


def nn_dot(a, b):
    return jnp.dot(a, b, preferred_element_type=jnp.float32)


def column_of(row):
    pieces = []
    eye = lax.broadcasted_iota(jnp.int32, (dim, dim), 0) == lax.broadcasted_iota(
        jnp.int32, (dim, dim), 1
    )
    for start in range(0, keys, dim):
        spread = jnp.broadcast_to(row[:, start : start + dim], (dim, dim))
        column = jnp.sum(jnp.where(eye, spread, 0.0), axis=1, keepdims=True)
        pieces.append(column[: min(dim, keys - start)])
    return jnp.concatenate(pieces, axis=0)


def merge(parts):
    best = functools.reduce(jnp.maximum, [a[0:1] for a in parts])
    factors = [jnp.exp2(a[0:1] - best) for a in parts]
    total = sum(a[1:2] * f for a, f in zip(parts, factors))
    moment = sum(a[2:3] * f for a, f in zip(parts, factors))
    return best, total, moment


def kernel(
    q_ref,
    g_ref,
    k_ref,
    v_ref,
    table_hbm,
    gap_hbm,
    order_hbm,
    dq_got,
    dk_hbm,
    dv_hbm,
    db_hbm,
    dk_out,
    dv_out,
    db_out,
    table_ref,
    gap_ref,
    order_ref,
    q_all,
    g_all,
    k_all,
    v_all,
    k_turned,
    gap_rows,
    gap_cols,
    bias_cols,
    key_pos,
    query_pos,
    s_all,
    dp_all,
    state,
    stats,
    stats_got,
    p_low,
    ds_low,
    dq_all,
    held,
    dk_sum,
    dv_sum,
    ds_sum,
    kv_low,
    kv_got,
    db_own,
    db_got,
    local_sem,
    store_sem,
    gap_send,
    gap_recv,
    k_send,
    k_recv,
    v_send,
    v_recv,
    q_send,
    q_recv,
    g_send,
    g_recv,
    st_send,
    st_recv,
    dq_send,
    dq_recv,
    held_recv,
    on_send,
    dkv_send,
    dkv_recv,
    db_send,
    db_recv,
):
    row = lax.axis_index("row")
    col = lax.axis_index("col")
    depth = lax.axis_index("depth")
    z_lo = row // 8
    x = (row // 2) % 4
    core = row % 2
    z = depth * 4 + z_lo
    member = col // 2
    parity = col % 2
    other = (core + member) % 2
    own_row = col == 0
    dq_self = (member == 0) & (col == z_lo)

    def shift(j):
        return (parity + (1 if j in (1, 2) else 0)) % 2

    def at(step, xx):
        there = (z + step + 8) % 8
        return ((there % 4) * 8 + xx * 2 + other, col, there // 4)

    def slot_x(s):
        return (x + shift(s // 2) + 2 * (s % 2)) % 4

    def beside(d):
        return (z_lo * 8 + ((x + d) % 4) * 2 + core, col, depth)

    def peer(a, b):
        return (row, (col + a) % 4, (depth + b) % 2)

    loads = [
        pltpu.make_async_copy(src, dst, local_sem.at[n])
        for n, (src, dst) in enumerate(
            (
                (k_ref, k_all.at[0]),
                (v_ref, v_all.at[0]),
                (gap_hbm, gap_ref),
                (table_hbm, table_ref),
                (order_hbm, order_ref),
            )
        )
    ]
    for copy in loads:
        copy.start()

    barrier = pltpu.get_barrier_semaphore()

    def greet(device):
        pl.semaphore_signal(barrier, inc=1, device_id=device, device_id_type=MESH)

    for n in range(8):
        from_col, from_depth = n // 2, n % 2
        head_core = (core + from_col // 2) % 2

        @pl.when(jnp.logical_not(dq_self & (from_col == col) & (depth == from_depth)))
        def _(device=(col * 8 + x * 2 + head_core, from_col, from_depth)):
            greet(device)

    for n in (5, 7, 3, 4, 1, 6, 2):
        greet(peer(n // 2, n % 2))
    for d in (2, 1, 3):
        greet(beside(d))
    for step, j in ((2, 3), (-2, 3), (1, 1), (-1, 2), (0, 0)):
        for i in range(2):
            device = at(step, (x + shift(j) + 2 * i) % 4)
            if step == 0 and i == 0:

                @pl.when(jnp.logical_not(own_row))
                def _(device=device):
                    greet(device)

            else:
                greet(device)
    loads[2].wait()
    gap_rows[0] = jnp.zeros((1, 640), jnp.float32)
    gap_rows[0, 0:1, 0:keys] = gap_ref[...].astype(jnp.float32).reshape(1, keys)

    pl.semaphore_wait(
        barrier,
        28 - own_row.astype(jnp.int32) - dq_self.astype(jnp.int32),
    )

    def remote(src, dst, send_sem, recv_sem, device):
        return pltpu.make_async_remote_copy(
            src_ref=src,
            dst_ref=dst,
            send_sem=send_sem,
            recv_sem=recv_sem,
            device_id=device,
            device_id_type=MESH,
        )

    def gap_copy(a):
        return remote(
            gap_rows.at[0], gap_rows.at[4 - a], gap_send.at[a - 1], gap_recv.at[3 - a], peer(a, 0)
        )

    def own_copy(a, h, src, dst, send, recv):
        part = pl.ds(h * half_keys, half_keys)
        return remote(
            src.at[part, :],
            dst.at[4 - a, part, :],
            send.at[a - 1, h],
            recv.at[3 - a, h],
            peer(a, 0),
        )

    def pass_copy(a, h, dst, send, recv):
        part = pl.ds(h * half_keys, half_keys)
        return remote(
            dst.at[4 - a, part, :], dst.at[2, part, :], send.at[1, h], recv.at[1, h], peer(a, 0)
        )

    gaps = [gap_copy(a) for a in (1, 3, 2)]
    passed, direct, onward = [], [], []
    for h in range(2):
        passed.append(own_copy(1, h, k_ref, k_all, k_send, k_recv))
        passed.append(own_copy(3, h, v_ref, v_all, v_send, v_recv))
        direct.append(own_copy(3, h, k_ref, k_all, k_send, k_recv))
        direct.append(own_copy(1, h, v_ref, v_all, v_send, v_recv))
        onward.append(pass_copy(1, h, k_all, k_send, k_recv))
        onward.append(pass_copy(3, h, v_all, v_send, v_recv))
    for copy in passed:
        copy.start()

    def send_rows(src, dst, send_sem, recv_sem, step, j):
        for i in range(2):
            target = at(step, (x + 3 * shift(j) + 2 * i) % 4)
            src_part = src.at[:, pl.ds(pl.multiple_of(target[0] * dim, dim), dim)]
            dst_part = dst.at[pl.ds((j * 2 + i) * rows, rows), :]
            away = remote(src_part, dst_part, send_sem, recv_sem.at[j], target)
            if step == 0 and i == 0:

                @pl.when(own_row)
                def _(src_part=src_part, dst_part=dst_part):
                    pltpu.make_async_copy(src_part, dst_part, recv_sem.at[j]).start()

                @pl.when(jnp.logical_not(own_row))
                def _(away=away):
                    away.start()

            else:
                away.start()

    send_rows(q_ref, q_all, q_send, q_recv, 0, 0)
    send_rows(g_ref, g_all, g_send, g_recv, 0, 0)
    for copy in gaps:
        copy.start()
    send_rows(q_ref, q_all, q_send, q_recv, -1, 1)
    send_rows(g_ref, g_all, g_send, g_recv, -1, 1)
    send_rows(q_ref, q_all, q_send, q_recv, 1, 2)
    send_rows(g_ref, g_all, g_send, g_recv, 1, 2)
    send_rows(q_ref, q_all, q_send, q_recv, -2, 3)
    send_rows(g_ref, g_all, g_send, g_recv, 2, 3)
    for copy in direct:
        copy.start()

    for n in (0, 1, 3, 4):
        loads[n].wait()

    lane = lax.broadcasted_iota(jnp.int32, (1, queries), 1)
    half = rows // 2
    pos = jnp.zeros((1, queries), jnp.int32)
    for s in range(slots):
        r = ((z_lo + z_steps[s // 2]) % 4) * 8 + slot_x(s) * 2 + other
        for b in range(2):
            low = s * rows + b * half
            inside = (lane >= low) & (lane < low + half)
            pos = jnp.where(inside, order_ref[2 * r + b] * half + lane - low, pos)
    query_pos[...] = pos
    within = lax.broadcasted_iota(jnp.int32, (keys, dim), 0)
    for b in range(blocks):
        key_pos[b * keys : (b + 1) * keys, :] = within + (((col + b) % 4) * 2 + depth) * keys
    level = lax.broadcasted_iota(jnp.int32, (1, levels), 1).astype(jnp.float32)
    table = table_ref[pl.ds(row, 1), :]

    def fill_bias(b):
        start = b * keys
        column = column_of(gap_rows[b, 0:1, :])
        gap_cols[start : start + keys, :] = jnp.broadcast_to(column, (keys, dim))
        bias = jnp.sum(jnp.where(column == level, table, 0.0), axis=1, keepdims=True)
        bias_cols[start : start + keys, :] = jnp.broadcast_to(bias * log2e, (keys, dim))

    def turn(b):
        k_turned[b] = k_all[b].astype(jnp.float32).T.astype(jnp.bfloat16)

    fill_bias(0)
    fresh = jnp.zeros((8, queries), jnp.float32)
    state[0] = fresh + floor_value
    state[1] = fresh
    state[2] = fresh
    turn(0)

    for come, go in zip(passed, onward):
        come.wait_recv()
        go.start()
    for copy in gaps:
        copy.wait_recv()
    for b in (3, 1, 2):
        fill_bias(b)

    def wait_group(buffer, sem, j):
        part = buffer.at[pl.ds(j * 2 * rows, 2 * rows), :]
        pltpu.make_async_copy(part, part, sem.at[j]).wait()

    def first_pass(c, b):
        lo, hi = cuts[c], cuts[c + 1]
        count = hi - lo
        part = slice(b * keys, (b + 1) * keys)
        s = nt_dot(k_all[b], q_all[lo:hi, :]) * (scale * log2e)
        s = s + wide(bias_cols[part, :], count)
        s = jnp.where(wide(key_pos[part, :], count) <= query_pos[:, lo:hi], s, masked_value)
        s_all[part, lo:hi] = s
        dp = nt_dot(v_all[b], g_all[lo:hi, :])
        dp_all[part, lo:hi] = dp
        before = state[0, :, lo:hi]
        best = jnp.maximum(before, fold(s, jnp.max))
        factor = jnp.exp2(before - best)
        w = jnp.exp2(s.reshape(keys // 8, 8, count) - best[None])
        wd = w * dp.reshape(keys // 8, 8, count)
        state[0, :, lo:hi] = best
        state[1, :, lo:hi] = state[1, :, lo:hi] * factor + jnp.sum(w, axis=0)
        state[2, :, lo:hi] = state[2, :, lo:hi] * factor + jnp.sum(wd, axis=0)

    def stat_copy(c):
        part = pl.ds(cuts[c], cuts[c + 1] - cuts[c])
        return remote(
            stats.at[:, part], stats_got.at[:, part], st_send.at[c], st_recv.at[c], peer(0, 1)
        )

    def close(c):
        lo, hi = cuts[c], cuts[c + 1]
        best = jnp.max(state[0, :, lo:hi], axis=0, keepdims=True)
        factor = jnp.exp2(state[0, :, lo:hi] - best)
        stats[0:1, lo:hi] = best
        stats[1:2, lo:hi] = jnp.sum(state[1, :, lo:hi] * factor, axis=0, keepdims=True)
        stats[2:3, lo:hi] = jnp.sum(state[2, :, lo:hi] * factor, axis=0, keepdims=True)
        stat_copy(c).start()

    wait_group(q_all, q_recv, 0)
    wait_group(g_all, g_recv, 0)
    wait_group(q_all, q_recv, 1)
    wait_group(g_all, g_recv, 1)
    first_pass(0, 0)
    for copy in direct:
        copy.wait_recv()
    first_pass(0, 1)
    first_pass(0, 3)
    for j in (2, 3):
        wait_group(q_all, q_recv, j)
        wait_group(g_all, g_recv, j)
    for b in (0, 1, 3):
        first_pass(1, b)
    for copy in onward:
        copy.wait_recv()
    for c in range(chunks):
        first_pass(c, 2)
        close(c)
    for b in (2, 3, 1):
        turn(b)

    def kv_copy(n, a):
        return remote(
            kv_low.at[n], kv_got.at[n], dkv_send.at[n], dkv_recv.at[n], peer(a, 0)
        )

    returns = [kv_copy(n, a) for n, a in enumerate((1, 3, 3, 1, 1, 3))]

    def low(total, b, factor):
        return (total[b * keys : (b + 1) * keys, :] * factor).astype(jnp.bfloat16)

    def slot_d(s):
        return (shift(s // 2) + 2 * (s % 2)) % 4

    def onto(s, src):
        head_x = (x + 4 - slot_d(s)) % 4
        place = (head_x % 2) * 2 + core
        dst = dq_got.at[place, pl.ds(pl.multiple_of(depth * rows, rows), rows), :]
        target = (((z_lo + z_steps[s // 2]) % 4) * 8 + x * 2 + other, z_lo, head_x // 2)
        mine = dq_self & (head_x // 2 == depth) if s // 2 == 0 else None
        return remote(src, dst, on_send.at[s], dq_recv.at[place], target), mine, place, dst

    def send_on(s, src):
        away, mine, place, dst = onto(s, src)
        if mine is None:
            away.start()
        else:

            @pl.when(mine)
            def _():
                pltpu.make_async_copy(src, dst, dq_recv.at[place]).start()

            @pl.when(jnp.logical_not(mine))
            def _():
                away.start()

    def hand_on(s):
        def go():
            pltpu.make_async_copy(held.at[s], held.at[s], held_recv.at[s]).wait()
            send_on(s, held.at[s])

        if s % 2:
            go()
        else:
            pl.when(shift(s // 2) == 1)(go)

    def factors(c):
        lo, hi = cuts[c], cuts[c + 1]
        stat_copy(c).wait()
        best, total, moment = merge([stats[0:3, lo:hi], stats_got[0:3, lo:hi]])
        return best + jnp.log(total) * log2e, moment / total

    def score_grads(c, b, lse, delta):
        lo, hi = cuts[c], cuts[c + 1]
        part = slice(b * keys, (b + 1) * keys)
        p = jnp.exp2(s_all[part, lo:hi] - lse)
        ds = p * (dp_all[part, lo:hi] - delta)
        ds_lanes = sum(ds[:, n * dim : (n + 1) * dim] for n in range((hi - lo) // dim))
        if c == 0:
            ds_sum[part, :] = ds_lanes
        else:
            ds_sum[part, :] += ds_lanes
        p_low[part, lo:hi] = p.astype(jnp.bfloat16)
        ds_low[part, lo:hi] = ds.astype(jnp.bfloat16)
        return nn_dot(k_turned[b], ds_low[part, lo:hi])

    def key_grads(b):
        part = slice(b * keys, (b + 1) * keys)
        dk_sum[part, :] = nn_dot(ds_low[part, :], q_all[...])
        dv_sum[part, :] = nn_dot(p_low[part, :], g_all[...])

    def send_dq(c, dq):
        dq_all[cuts[c] : cuts[c + 1], :] = (dq.T * scale).astype(jnp.bfloat16)
        for s in range(cuts[c] // rows, cuts[c + 1] // rows):
            src = dq_all.at[pl.ds(s * rows, rows), :]
            aside = remote(src, held.at[s], dq_send, held_recv.at[s], beside(slot_d(s)))
            if s % 2:
                aside.start()
            else:

                @pl.when(shift(s // 2) == 0)
                def _(s=s, src=src):
                    send_on(s, src)

                @pl.when(shift(s // 2) == 1)
                def _(aside=aside):
                    aside.start()

    def send_kv(n, total, b, factor):
        kv_low[n] = low(total, b, factor)
        returns[n].start()

    near = factors(0)
    dq_near = score_grads(0, 2, *near)
    rest = factors(1)
    dq_rest = score_grads(1, 2, *rest)
    key_grads(2)
    send_kv(0, dk_sum, 2, scale)
    send_kv(1, dv_sum, 2, 1.0)
    for b in (3, 1, 0):
        dq_near = dq_near + score_grads(0, b, *near)
    send_dq(0, dq_near)
    for b in (3, 1, 0):
        dq_rest = dq_rest + score_grads(1, b, *rest)
    send_dq(1, dq_rest)
    key_grads(3)
    send_kv(2, dk_sum, 3, scale)
    key_grads(1)
    send_kv(3, dv_sum, 1, 1.0)
    column = jnp.sum(ds_sum[...], axis=1, keepdims=True)
    by_level = jnp.where(gap_cols[:, 0:levels] == level, column, 0.0)
    db_own[...] = jnp.zeros_like(db_own)
    db_own[0:1, 0:levels] = jnp.sum(by_level, axis=0, keepdims=True)
    biases = [
        remote(db_own, db_got.at[n - 1], db_send.at[n - 1], db_recv.at[n - 1], peer(n // 2, n % 2))
        for n in range(1, 8)
    ]
    for copy in biases:
        copy.start()

    for s in range(3):
        hand_on(s)
    key_grads(0)

    returns[0].wait_recv()
    kv_low[4] = (dk_sum[keys : 2 * keys, :] * scale + kv_got[0].astype(jnp.float32)).astype(
        jnp.bfloat16
    )
    returns[4].start()
    returns[1].wait_recv()
    kv_low[5] = (dv_sum[3 * keys : 4 * keys, :] + kv_got[1].astype(jnp.float32)).astype(
        jnp.bfloat16
    )
    returns[5].start()
    for s in range(3, slots):
        hand_on(s)

    stores = [
        pltpu.make_async_copy(src, dst, store_sem.at[n])
        for n, (src, dst) in enumerate(((dk_out, dk_hbm), (dv_out, dv_hbm), (db_out, db_hbm)))
    ]
    returns[2].wait_recv()
    returns[4].wait_recv()
    dk_out[...] = (
        dk_sum[0:keys, :] * scale + kv_got[2].astype(jnp.float32) + kv_got[4].astype(jnp.float32)
    )
    stores[0].start()
    returns[3].wait_recv()
    returns[5].wait_recv()
    dv_out[...] = (
        dv_sum[0:keys, :] + kv_got[3].astype(jnp.float32) + kv_got[5].astype(jnp.float32)
    )
    stores[1].start()
    for copy in biases:
        copy.wait()
    db_out[...] = db_own[0:1, 0:levels] + sum(db_got[n, 0:1, 0:levels] for n in range(7))
    stores[2].start()

    for head in range(4):
        both = dq_got.at[head]
        pltpu.make_async_copy(both, both, dq_recv.at[head]).wait()

    def drain(buffer, sem, short):
        @pl.when(short)
        def _():
            part = buffer.at[pl.ds(0, queries - rows), :]
            pltpu.make_async_copy(part, part, sem).wait()

        @pl.when(jnp.logical_not(short))
        def _():
            pltpu.make_async_copy(buffer, buffer, sem).wait()

    drain(q_all, q_send, own_row)
    drain(g_all, g_send, own_row)
    part = dq_all.at[pl.ds(0, 6 * rows), :]
    pltpu.make_async_copy(part, part, dq_send).wait()
    for s in range(slots):
        away, mine, _, _ = onto(s, held.at[s])
        if mine is None:
            away.wait_send()
        else:
            pl.when(jnp.logical_not(mine))(away.wait_send)

    for copy in stores:
        copy.wait()
    for copy in gaps + passed + direct + onward + returns:
        copy.wait_send()


def place_kernel(dq, dk, dv, db, dq_out, dk_out, dv_out, db_out):
    for head in range(4):
        dq_out[:, head * dim : (head + 1) * dim] = dq[head, 0:rows, :].astype(
            jnp.float32
        ) + dq[head, rows : 2 * rows, :].astype(jnp.float32)
    dk_out[...] = dk[...]
    dv_out[...] = dv[...]
    db_out[...] = db[...]


def per_device(queries_in, key_states, value_states, grad_output, bias_table, gap_bucket, order):
    vmem = pl.BlockSpec(memory_space=pltpu.VMEM)
    hbm = pl.BlockSpec(memory_space=pltpu.HBM)
    low, full = jnp.bfloat16, jnp.float32
    dma = pltpu.SemaphoreType.DMA
    outs = (
        jax.ShapeDtypeStruct((rows, 4 * dim), full),
        jax.ShapeDtypeStruct((keys, dim), full),
        jax.ShapeDtypeStruct((keys, dim), full),
        jax.ShapeDtypeStruct((1, levels), full),
    )
    results = pl.pallas_call(
        kernel,
        out_shape=(jax.ShapeDtypeStruct((4, 2 * rows, dim), low),) + outs[1:],
        in_specs=[
            hbm,
            hbm,
            hbm,
            hbm,
            hbm,
            hbm,
            hbm,
        ],
        out_specs=(hbm, hbm, hbm, hbm),
        scratch_shapes=[pltpu.VMEM(a.shape, full) for a in outs[1:]]
        + [
            pltpu.VMEM((32, levels), full),
            pltpu.VMEM((keys,), jnp.int32),
            pltpu.SMEM((64,), jnp.int32),
            pltpu.VMEM((queries, dim), low),
            pltpu.VMEM((queries, dim), low),
            pltpu.VMEM((blocks, keys, dim), low),
            pltpu.VMEM((blocks, keys, dim), low),
            pltpu.VMEM((blocks, dim, keys), low),
            pltpu.VMEM((blocks, 1, 640), full),
            pltpu.VMEM((all_keys, dim), full),
            pltpu.VMEM((all_keys, dim), full),
            pltpu.VMEM((all_keys, dim), jnp.int32),
            pltpu.VMEM((1, queries), jnp.int32),
            pltpu.VMEM((all_keys, queries), full),
            pltpu.VMEM((all_keys, queries), full),
            pltpu.VMEM((3, 8, queries), full),
            pltpu.VMEM((8, queries), full),
            pltpu.VMEM((8, queries), full),
            pltpu.VMEM((all_keys, queries), low),
            pltpu.VMEM((all_keys, queries), low),
            pltpu.VMEM((queries, dim), low),
            pltpu.VMEM((slots, rows, dim), low),
            pltpu.VMEM((all_keys, dim), full),
            pltpu.VMEM((all_keys, dim), full),
            pltpu.VMEM((all_keys, dim), full),
            pltpu.VMEM((6, keys, dim), low),
            pltpu.VMEM((6, keys, dim), low),
            pltpu.VMEM((8, dim), full),
            pltpu.VMEM((7, 8, dim), full),
            dma((5,)),
            dma((3,)),
            dma((3,)),
            dma((3,)),
            dma((3, 2)),
            dma((3, 2)),
            dma((3, 2)),
            dma((3, 2)),
            dma(()),
            dma((4,)),
            dma(()),
            dma((4,)),
            dma((chunks,)),
            dma((chunks,)),
            dma(()),
            dma((4,)),
            dma((slots,)),
            dma((slots,)),
            dma((6,)),
            dma((6,)),
            dma((7,)),
            dma((7,)),
        ],
        compiler_params=pltpu.CompilerParams(
            collective_id=0, has_side_effects=True, vmem_limit_bytes=60 * 1024 * 1024
        ),
        cost_estimate=pl.CostEstimate(
            flops=10 * all_keys * queries * dim,
            bytes_accessed=8 * queries * dim,
            transcendentals=2 * all_keys * queries,
        ),
    )(
        queries_in,
        grad_output,
        key_states,
        value_states,
        bias_table,
        gap_bucket,
        order,
    )
    return pl.pallas_call(
        place_kernel,
        out_shape=outs,
        in_specs=[vmem] * 4,
        out_specs=(vmem,) * 4,
    )(*results)


def solution(mesh):
    placed = (
        P("row", None),
        P(("col", "depth"), "row"),
        P(("col", "depth"), "row"),
        P("row", None),
        P(),
        P(("col", "depth")),
        P(),
    )
    return jax.shard_map(
        per_device,
        mesh=mesh,
        in_specs=placed,
        out_specs=(
            P("row", ("col", "depth")),
            P(("col", "depth"), "row"),
            P(("col", "depth"), "row"),
            P("row", None),
        ),
        check_vma=False,
    )
```
